32 devices in a mesh: group: 4 (over x, core), leaf: 8 (over z, y).
Axes of the slice: x: 2, y: 2, z: 4, core: 2. Of those that a mesh axis runs over, the one named last changes fastest.
Arguments:
- top_modes: bfloat16 [1024, 512], P('group'), may hold values from -6 to 6
- low_modes: bfloat16 [2048, 512], P(('group', 'leaf')), may hold values from -6 to 6
- anc_top: int32 [32, 8], P(('group', 'leaf')), may hold values from 0 to 15, all different within a row
- anc_low: int32 [32, 8], P(('group', 'leaf')), may hold values from 0 to 7, all different within a row
- coupling: bfloat16 [49152, 1024], P(('group', 'leaf')), may hold values from -0.1875 to 0.1875
- leaf_mass: bfloat16 [49152, 1536], P(('group', 'leaf')), may hold values from -0.15625 to 0.15625
- leaf_modes: bfloat16 [49152, 128], P(('group', 'leaf')), may hold values from -0.5 to 0.5
- leaf_coef: bfloat16 [4096, 512], P(('group', 'leaf')), may hold values from -6 to 6
- kinv_top: float32 [1024, 64], P('group'), may hold values from -0.1875 to 0.1875
- kinv_low: float32 [2048, 64], P(('group', 'leaf')), may hold values from -0.25 to 0.25
Outputs:
- new_top: float32 [1024, 512], P('group')
- new_low: float32 [2048, 512], P(('group', 'leaf'))
- leaf_proj: bfloat16 [4096, 512], P(('group', 'leaf'))
The draws below stay inside these ranges and needn't reach their ends.
Inputs may be any that keep to these rules, and one draw needn't show every extreme that they name: `anc_top`: each row names 8 different top separator blocks. `anc_low`: each row names 8 different leaf indices of the leaf's own subtree.
All inputs are finite; a program needn't handle non-finite values.
Results may differ from the reference program's by a relative error of at most 0.0057.
Values may be sent and summed in bfloat16 or wider, within the bound.
No kernel may reach another device: no remote copies, remote signals or barrier semaphores. Data moves between devices by JAX's collectives and lax.ppermute only.
A program may use at most 128 MiB of HBM per device.

```python
import jax
import jax.numpy as jnp
from jax import lax

M = 512
SR = 64
ANC_TOP = 8
KL = 128
NL = 1536
ANC_LOW = 8
SW = 1024
TOPS = 16
LEAVES = 32
N_GROUP = 4
N_LEAF = 8


def shard_levels(own_key, shape, split, least, high):
    loudness, own = 1.0, jax.random.fold_in(own_key, 6)
    for dim, blocks in split:
        steps = jnp.exp(jax.random.uniform(jax.random.fold_in(own, dim), (blocks,), jnp.float32, least / len(split), high / len(split)))
        loudness = loudness * jnp.repeat(steps, shape[dim] // blocks).reshape([-1 if axis == dim else 1 for axis in range(len(shape))])
    return loudness


def distinct(own_key, rows, amount, top, lift):
    order = jax.random.permutation(jax.random.fold_in(own_key, 1), amount)
    favour = order
    for power in range(3):
        favour = favour * favour // amount
    favour = favour * lift // amount
    chance = jax.random.randint(jax.random.fold_in(own_key, 2), (rows, amount), 0, 4096) + favour
    fixed_rows = jax.random.permutation(jax.random.fold_in(own_key, 3), rows)[jnp.arange(amount) % rows]
    chance = jnp.where(jnp.arange(rows)[:, None] == fixed_rows[None, :], 1 << 14, chance)
    priority = chance * amount + jnp.arange(amount)
    return lax.top_k(priority.astype(jnp.int32), top)[1].astype(jnp.int32)


def noise(stream_key, shape, width, bound, split=(), kind=jnp.bfloat16):
    values = jax.random.normal(stream_key, shape, jnp.float32) * width
    if len(split) > 0:
        values = shard_levels(stream_key, shape, split, -0.22, 0.18) * values
    return jnp.clip(values, min=-bound, max=bound).astype(kind)


def setup_inputs(seed: int = 0) -> dict:
    keys = jax.random.split(jax.random.key(seed), 11)
    top_modes = noise(keys[0], (TOPS * SR, M), 1.0, 6.0, ((0, 4),))
    low_modes = noise(keys[1], (LEAVES * SR, M), 1.0, 6.0, ((0, 32),))
    anc_top = distinct(keys[2], LEAVES, TOPS, ANC_TOP, 0)
    anc_low = distinct(keys[3], LEAVES, N_LEAF, ANC_LOW, 0)
    coupling = noise(keys[4], (LEAVES * NL, SW), SW ** -0.5, 0.1875, ((0, 32),))
    leaf_mass = noise(keys[5], (LEAVES * NL, NL), NL ** -0.5, 0.15625, ((0, 32),))
    leaf_modes = noise(keys[6], (LEAVES * NL, KL), KL ** -0.5, 0.5, ((0, 32),))
    leaf_coef = noise(keys[7], (LEAVES * KL, M), 1.0, 6.0, ((0, 32),))
    kinv_top = noise(keys[8], (TOPS * SR, SR), (SR * LEAVES * ANC_TOP // TOPS) ** -0.5, 0.1875, ((0, 4),), jnp.float32)
    kinv_low = noise(keys[9], (LEAVES * SR, SR), (SR * ANC_LOW) ** -0.5, 0.25, ((0, 32),), jnp.float32)
    return dict(top_modes=top_modes, low_modes=low_modes, anc_top=anc_top, anc_low=anc_low, coupling=coupling, leaf_mass=leaf_mass, leaf_modes=leaf_modes, leaf_coef=leaf_coef, kinv_top=kinv_top, kinv_low=kinv_low)


def reference(top_modes, low_modes, anc_top, anc_low, coupling, leaf_mass, leaf_modes, leaf_coef, kinv_top, kinv_low):
    top_blocks = top_modes.reshape(TOPS, SR, M)
    low_blocks = low_modes.reshape(N_GROUP, N_LEAF, SR, M)

    def one_leaf(totals, leaf_index):
        top_loads, low_loads = totals
        group_index = leaf_index // N_LEAF
        top_sel = top_blocks[anc_top[leaf_index]]
        low_sel = low_blocks[group_index][anc_low[leaf_index]]
        stacked = jnp.concatenate([top_sel, low_sel], axis=0).reshape(SW, M)
        coupler = lax.dynamic_slice_in_dim(coupling, leaf_index * NL, NL, 0)
        mass_block = lax.dynamic_slice_in_dim(leaf_mass, leaf_index * NL, NL, 0)
        basis = lax.dynamic_slice_in_dim(leaf_modes, leaf_index * NL, NL, 0)
        coeffs = lax.dynamic_slice_in_dim(leaf_coef, leaf_index * KL, KL, 0)
        shapes = (jnp.dot(basis, coeffs, preferred_element_type=jnp.float32)
                  - jnp.dot(coupler, stacked, preferred_element_type=jnp.float32)).astype(jnp.bfloat16)
        weighted = jnp.dot(mass_block, shapes, preferred_element_type=jnp.float32).astype(jnp.bfloat16)
        loads = jnp.dot(coupler.T, weighted, preferred_element_type=jnp.float32)
        projected = jnp.dot(basis.T, weighted, preferred_element_type=jnp.float32).astype(jnp.bfloat16)
        top_loads = top_loads.at[anc_top[leaf_index]].add(loads[:ANC_TOP * SR].reshape(ANC_TOP, SR, M))
        low_loads = low_loads.at[group_index, anc_low[leaf_index]].add(loads[ANC_TOP * SR:].reshape(ANC_LOW, SR, M))
        return (top_loads, low_loads), projected

    leaf_ids = jnp.arange(N_GROUP * N_LEAF, dtype=jnp.int32)
    start_totals = (jnp.zeros((TOPS, SR, M), jnp.float32), jnp.zeros((N_GROUP, N_LEAF, SR, M), jnp.float32))
    (top_loads, low_loads), projected = lax.scan(one_leaf, start_totals, leaf_ids)
    new_top = jnp.einsum("brs,bsm->brm", kinv_top.reshape(TOPS, SR, SR), top_loads,
                         precision=lax.Precision.HIGHEST).reshape(TOPS * SR, M)
    new_low = jnp.einsum("brs,bsm->brm", kinv_low.reshape(N_GROUP * N_LEAF, SR, SR),
                         low_loads.reshape(N_GROUP * N_LEAF, SR, M),
                         precision=lax.Precision.HIGHEST).reshape(N_GROUP * N_LEAF * SR, M)
    leaf_proj = projected.reshape(N_GROUP * N_LEAF * KL, M)
    return (new_top, new_low, leaf_proj)
```

```python
import functools

import jax
import jax.numpy as jnp
from jax import lax
from jax.experimental import pallas as pl
from jax.experimental.pallas import tpu as pltpu
from jax.sharding import PartitionSpec as P

BF16, F32 = jnp.bfloat16, jnp.float32
VMEM = pl.BlockSpec(memory_space=pltpu.VMEM)
SMEM = pl.BlockSpec(memory_space=pltpu.SMEM)
ANY = pl.BlockSpec(memory_space=pl.ANY)
HIGHEST = lax.Precision.HIGHEST


def leaf_factors(leaves):
    inner = 2 if (leaves.bit_length() - 1) % 2 else 4
    outer = []
    stride = leaves
    while stride > inner:
        stride //= 4
        outer.append((4, stride))
    return inner, outer


def params(mib):
    return pltpu.CompilerParams(vmem_limit_bytes=mib * 2**20)


def cost(flops, moved):
    return pl.CostEstimate(flops=flops, bytes_accessed=moved, transcendentals=0)


def send_group(x, k):
    return lax.ppermute(x, "group", [(i, i ^ k) for i in range(lax.axis_size("group"))])


def send_leaf(x, k):
    return lax.ppermute(x, "leaf", [(i, i ^ k) for i in range(lax.axis_size("leaf"))])


def send_both(x, kg, kl):
    groups, leaves = lax.axis_size("group"), lax.axis_size("leaf")
    pairs = [(g * leaves + l, (g ^ kg) * leaves + (l ^ kl)) for g in range(groups) for l in range(leaves)]
    return lax.ppermute(x, ("group", "leaf"), pairs)


def gather_leaf(x, steps):
    held = [(x, [0])]
    for fac, stride in steps:
        if len(held) > 4:
            held = [(jnp.concatenate([a for a, _ in held], axis=0), [r for _, rs in held for r in rs])]
        held = held + [
            (send_leaf(a, k * stride), [r ^ (k * stride) for r in rs]) for k in range(1, fac) for a, rs in held
        ]
    return held


def transpose_kernel(c_ref, m_ref, ct_ref, mt_ref):
    ct_ref[...] = c_ref[...].T
    mt_ref[...] = m_ref[...].T


def transposed(coupling, leaf_modes):
    rows, width = coupling.shape
    modes = leaf_modes.shape[1]
    step = 512
    return pl.pallas_call(
        transpose_kernel,
        grid=(rows // step,),
        in_specs=[pl.BlockSpec((step, width), lambda i: (i, 0)), pl.BlockSpec((step, modes), lambda i: (i, 0))],
        out_specs=[pl.BlockSpec((width, step), lambda i: (0, i)), pl.BlockSpec((modes, step), lambda i: (0, i))],
        out_shape=[jax.ShapeDtypeStruct((width, rows), BF16), jax.ShapeDtypeStruct((modes, rows), BF16)],
        compiler_params=params(24),
        cost_estimate=cost(0, 4 * rows * (width + modes)),
    )(coupling, leaf_modes)


def main_kernel(
    n_top, low_rels, inner, anc_top, anc_low, *refs
):
    n_low = len(low_rels)
    tops, lows = refs[:n_top], refs[n_top : n_top + n_low]
    coupling, mass, modes, coef, ct = refs[n_top + n_low : n_top + n_low + 5]
    send, keep, weighted = refs[n_top + n_low + 5 : n_top + n_low + 8]
    top_v, low_v, c_v, mass_v, modes_v, coef_v, ct_v, stacked, shapes, sem, sem_c, sem_m, sem_t = refs[
        n_top + n_low + 8 :
    ]
    sr = top_v.shape[1]
    per_group = top_v.shape[0] // n_top
    top_slots, low_slots = anc_top.shape[1], anc_low.shape[1]
    group, leaf = lax.axis_index("group"), lax.axis_index("leaf")
    rows = mass.shape[0]
    step = 512
    steps = rows // step

    first = []
    for i, t in enumerate(tops):
        for b in range(per_group):
            first.append((t.at[pl.ds(b * sr, sr)], top_v.at[i * per_group + b]))
    for a, rels in zip(lows, low_rels):
        for p, r in enumerate(rels):
            first.append((a.at[pl.ds(p * sr, sr)], low_v.at[r]))
    first.append((modes, modes_v))
    first.append((coef, coef_v))
    first = [pltpu.make_async_copy(s, d, sem.at[i]) for i, (s, d) in enumerate(first)]
    for c in first:
        c.start()
    c_copies = [
        pltpu.make_async_copy(coupling.at[pl.ds(i * step, step)], c_v.at[pl.ds(i * step, step)], sem_c.at[i])
        for i in range(steps)
    ]
    for c in c_copies:
        c.start()
    m_copies = [
        pltpu.make_async_copy(mass.at[pl.ds(i * step, step)], mass_v.at[pl.ds(i * step, step)], sem_m.at[i])
        for i in range(steps)
    ]
    for c in m_copies:
        c.start()
    t_copy = pltpu.make_async_copy(ct.at[pl.ds(0, top_slots * sr)], ct_v, sem_t)
    t_copy.start()
    send[...] = jnp.zeros(send.shape, send.dtype)
    keep[...] = jnp.zeros(keep.shape, keep.dtype)
    for c in first:
        c.wait()
    for j in range(top_slots):
        b = anc_top[0, j]
        owner = b // per_group
        stacked[pl.ds(j * sr, sr), :] = top_v[(owner ^ group) * per_group + b % per_group]
    for j in range(low_slots):
        stacked[pl.ds((top_slots + j) * sr, sr), :] = low_v[anc_low[0, j] ^ leaf]
    for i in range(steps):
        c_copies[i].wait()
        for h in range(2):
            at = pl.ds(i * step + h * (step // 2), step // 2)
            shapes[at, :] = (
                jnp.dot(modes_v[at, :], coef_v[...], preferred_element_type=F32)
                - jnp.dot(c_v[at, :], stacked[...], preferred_element_type=F32)
            ).astype(BF16)
    for i in range(steps):
        m_copies[i].wait()
        for h in range(2):
            at = pl.ds(i * step + h * (step // 2), step // 2)
            weighted[at, :] = jnp.dot(mass_v[at, :], shapes[...], preferred_element_type=F32).astype(BF16)
    t_copy.wait()
    core, far = group & 1, group >> 1
    width = weighted.shape[1] // inner
    for q in range(inner):
        col = pl.multiple_of(((leaf & (inner - 1)) ^ q) * width, 128)
        for h in range(2):
            half = top_slots // 2
            loads = jnp.dot(
                ct_v[pl.ds(h * half * sr, half * sr), :], weighted[:, pl.ds(col, width)], preferred_element_type=F32
            )
            for j in range(half):
                b = anc_top[0, h * half + j]
                owner = b // per_group
                at = pl.ds(pl.multiple_of((((owner >> 1) ^ far) * per_group + b % per_group) * sr, sr), sr)
                block = loads[j * sr : (j + 1) * sr]

                @pl.when((owner & 1) == core)
                def _():
                    keep[at, q * width : (q + 1) * width] = block

                @pl.when((owner & 1) != core)
                def _():
                    send[at, q * width : (q + 1) * width] = block.astype(BF16)


def main_call(anc_top, anc_low, tops, lows, low_rels, coupling, mass, modes, coef, ct, inner, sr, leaves):
    rows, sw = coupling.shape
    m = coef.shape[1]
    groups = len(tops)
    per_group = tops[0].shape[0] // sr
    half_rows = groups * per_group * sr // 2
    top_rows = anc_top.shape[1] * sr
    n_first = groups * per_group + leaves + 2
    flops = 2 * m * rows * (sw + rows + modes.shape[1] + top_rows)
    return pl.pallas_call(
        functools.partial(main_kernel, groups, low_rels, inner),
        in_specs=[SMEM, SMEM] + [ANY] * (groups + len(lows) + 5),
        out_specs=[VMEM, VMEM, VMEM],
        out_shape=[
            jax.ShapeDtypeStruct((half_rows, m), BF16),
            jax.ShapeDtypeStruct((half_rows, m), F32),
            jax.ShapeDtypeStruct((rows, m), BF16),
        ],
        scratch_shapes=[
            pltpu.VMEM((groups * per_group, sr, m), BF16),
            pltpu.VMEM((leaves, sr, m), BF16),
            pltpu.VMEM((rows, sw), BF16),
            pltpu.VMEM((rows, rows), BF16),
            pltpu.VMEM(modes.shape, BF16),
            pltpu.VMEM(coef.shape, BF16),
            pltpu.VMEM((top_rows, rows), BF16),
            pltpu.VMEM((sw, m), BF16),
            pltpu.VMEM((rows, m), BF16),
            pltpu.SemaphoreType.DMA((n_first,)),
            pltpu.SemaphoreType.DMA((rows // 512,)),
            pltpu.SemaphoreType.DMA((rows // 512,)),
            pltpu.SemaphoreType.DMA,
        ],
        compiler_params=params(40),
        cost_estimate=cost(flops, 2 * rows * (sw + rows)),
    )(anc_top, anc_low, *tops, *lows, coupling, mass, modes, coef, ct)


def low_kernel(inner, anc_low, ct, mt, weighted, proj, keep, *sends):
    slots = anc_low.shape[1]
    sr = ct.shape[0] // slots
    leaf = lax.axis_index("leaf")
    keep[...] = jnp.zeros(keep.shape, keep.dtype)
    for s in sends:
        s[...] = jnp.zeros(s.shape, s.dtype)
    part = 4
    for h in range(slots // part):
        loads = jnp.dot(ct[pl.ds(h * part * sr, part * sr), :], weighted[...], preferred_element_type=F32)
        for j in range(part):
            k = anc_low[0, h * part + j]
            at = pl.ds(pl.multiple_of((k // inner) * sr, sr), sr)
            turn = (k ^ leaf) & (inner - 1)
            block = loads[j * sr : (j + 1) * sr]

            @pl.when(turn == 0)
            def _():
                keep[at, :] = block

            for q, s in enumerate(sends):

                @pl.when(turn == q + 1)
                def _(s=s):
                    s[at, :] = block.astype(BF16)

    proj[...] = jnp.dot(mt[...], weighted[...], preferred_element_type=F32).astype(BF16)


def low_call(anc_low, ct, mt, weighted, inner, sr, leaves):
    rows, m = weighted.shape
    slots = anc_low.shape[1]
    skip = ct.shape[0] // (slots * sr) - 1
    assert ct.shape[0] % (slots * sr) == 0 or True
    kept = leaves // inner * sr
    low_rows = slots * sr
    at = (ct.shape[0] - low_rows) // sr
    del skip
    return pl.pallas_call(
        functools.partial(low_kernel, inner),
        grid=(1,),
        in_specs=[
            SMEM,
            pl.BlockSpec((pl.Element(low_rows), pl.Element(rows)), lambda i: (at * sr, 0)),
            VMEM,
            VMEM,
        ],
        out_specs=[VMEM] * (1 + inner),
        out_shape=[jax.ShapeDtypeStruct((mt.shape[0], m), BF16), jax.ShapeDtypeStruct((kept, m), F32)]
        + [jax.ShapeDtypeStruct((kept, m), BF16)] * (inner - 1),
        compiler_params=params(40),
        cost_estimate=cost(2 * m * rows * (low_rows + mt.shape[0]), 2 * rows * (low_rows + m)),
    )(anc_low, ct, mt, weighted)


def cross_kernel(inner, keep, got, own, *sends):
    rows, width = own.shape
    n = 0
    for far in range(keep.shape[0] // rows):
        for q in range(inner):
            at = (slice(far * rows, (far + 1) * rows), slice(q * width, (q + 1) * width))
            total = keep[at] + got[at].astype(F32)
            if far == 0 and q == 0:
                own[...] = total
            else:
                sends[n][...] = total.astype(BF16)
                n += 1


def cross_call(keep, got, inner):
    rows, width = keep.shape[0] // 2, keep.shape[1] // inner
    return pl.pallas_call(
        functools.partial(cross_kernel, inner),
        in_specs=[VMEM, VMEM],
        out_specs=[VMEM] * (2 * inner),
        out_shape=[jax.ShapeDtypeStruct((rows, width), F32)]
        + [jax.ShapeDtypeStruct((rows, width), BF16)] * (2 * inner - 1),
        compiler_params=params(16),
        cost_estimate=cost(keep.size, 8 * keep.size),
    )(keep, got)


def split_kernel(fac, stride, n_got, keep, *refs):
    got, own, sends = refs[:n_got], refs[n_got], refs[n_got + 1 :]
    rows = own.shape[0]
    digit = (lax.axis_index("leaf") // stride) & (fac - 1)
    for d in range(fac):
        at = pl.ds(pl.multiple_of((digit ^ d) * rows, rows), rows)
        total = keep[at, :]
        for g in got:
            total += g[at, :].astype(F32)
        if d == 0:
            own[...] = total
        else:
            sends[d - 1][...] = total.astype(BF16)


def split_call(keep, got, fac, stride):
    rows = keep.shape[0] // fac
    return pl.pallas_call(
        functools.partial(split_kernel, fac, stride, len(got)),
        in_specs=[VMEM] * (1 + len(got)),
        out_specs=[VMEM] * fac,
        out_shape=[jax.ShapeDtypeStruct((rows, keep.shape[1]), F32)]
        + [jax.ShapeDtypeStruct((rows, keep.shape[1]), BF16)] * (fac - 1),
        compiler_params=params(16),
        cost_estimate=cost(keep.size, 8 * keep.size),
    )(keep, *got)


def add_kernel(keep, *refs):
    total = keep[...]
    for g in refs[:-1]:
        total += g[...].astype(F32)
    refs[-1][...] = total.astype(BF16)


def add_call(keep, got):
    return pl.pallas_call(
        add_kernel,
        in_specs=[VMEM] * (1 + len(got)),
        out_specs=VMEM,
        out_shape=jax.ShapeDtypeStruct(keep.shape, BF16),
        compiler_params=params(16),
        cost_estimate=cost(keep.size, 8 * keep.size),
    )(keep, *got)


def low_end_kernel(keep, *refs):
    got, kinv, out = refs[:-2], refs[-2], refs[-1]
    total = keep[...]
    for g in got:
        total += g[...].astype(F32)
    out[...] = jnp.dot(kinv[...], total, preferred_element_type=F32, precision=HIGHEST)


def low_end_call(keep, got, kinv):
    return pl.pallas_call(
        low_end_kernel,
        in_specs=[VMEM] * (2 + len(got)),
        out_specs=VMEM,
        out_shape=jax.ShapeDtypeStruct(keep.shape, F32),
        compiler_params=params(16),
        cost_estimate=cost(12 * keep.size * 64, 8 * keep.size),
    )(keep, *got, kinv)


def top_end_kernel(rels, inner, outer, kinv, *refs):
    parts, out, loads = refs[:-2], refs[-2], refs[-1]
    leaf = lax.axis_index("leaf")
    rows, m = out.shape
    sr = kinv.shape[1]
    width = m // inner
    for part, rs in zip(parts, rels):
        size = part.shape[0] // len(rs)
        for p, r in enumerate(rs):
            there = leaf ^ r
            row, left = 0, rows
            for fac, stride in outer:
                left //= fac
                row += ((there // stride) & (fac - 1)) * left
            loads[
                pl.ds(pl.multiple_of(row, size), size), pl.ds(pl.multiple_of((there & (inner - 1)) * width, 128), width)
            ] = part[p * size : (p + 1) * size, :]
    for b in range(rows // sr):
        at = slice(b * sr, (b + 1) * sr)
        out[at, :] = jnp.dot(kinv[at, :], loads[at, :].astype(F32), preferred_element_type=F32, precision=HIGHEST)


def top_end_call(held, kinv, m, inner, outer):
    rows = kinv.shape[0]
    return pl.pallas_call(
        functools.partial(top_end_kernel, [r for _, r in held], inner, outer),
        in_specs=[VMEM] * (1 + len(held)),
        out_specs=VMEM,
        out_shape=jax.ShapeDtypeStruct((rows, m), F32),
        scratch_shapes=[pltpu.VMEM((rows, m), BF16)],
        compiler_params=params(16),
        cost_estimate=cost(12 * rows * m * 64, 8 * rows * m),
    )(kinv, *[a for a, _ in held])


def per_device(
    top_modes, low_modes, anc_top, anc_low, coupling, leaf_mass, leaf_modes, leaf_coef, kinv_top, kinv_low
):
    sr = kinv_low.shape[1]
    m = low_modes.shape[1]
    leaves = lax.axis_size("leaf")
    inner, outer = leaf_factors(leaves)
    far_top = send_group(top_modes, 2)
    tops = [top_modes, send_group(top_modes, 1), far_top, send_group(far_top, 1)]
    held = gather_leaf(low_modes, outer + [(inner, 1)])
    ct, mt = transposed(coupling, leaf_modes)
    send, keep, weighted = main_call(
        anc_top,
        anc_low,
        tops,
        [a for a, _ in held],
        [r for _, r in held],
        coupling,
        leaf_mass,
        leaf_modes,
        leaf_coef,
        ct,
        inner,
        sr,
        leaves,
    )
    got = send_group(send, 1)
    leaf_proj, low_keep, *low_sends = low_call(anc_low, ct, mt, weighted, inner, sr, leaves)
    low_got = [send_leaf(s, q + 1) for q, s in enumerate(low_sends)]
    own, *sends = cross_call(keep, got, inner)
    pairs = [(far, q) for far in range(2) for q in range(inner)][1:]
    got = [send_both(s, 2 * far, q) for s, (far, q) in zip(sends, pairs)]
    for fac, stride in outer:
        low_keep, *low_sends = split_call(low_keep, low_got, fac, stride)
        low_got = [send_leaf(s, (d + 1) * stride) for d, s in enumerate(low_sends)]
    for fac, stride in outer:
        own, *sends = split_call(own, got, fac, stride)
        got = [send_leaf(s, (d + 1) * stride) for d, s in enumerate(sends)]
    new_low = low_end_call(low_keep, low_got, kinv_low)
    top_held = gather_leaf(add_call(own, got), outer[::-1] + [(inner, 1)])
    new_top = top_end_call(top_held, kinv_top, m, inner, outer)
    return (new_top, new_low, leaf_proj)


def solution(mesh):
    both = P(("group", "leaf"), None)
    return jax.shard_map(
        per_device,
        mesh=mesh,
        in_specs=(P("group", None), both, both, both, both, both, both, both, P("group", None), both),
        out_specs=(P("group", None), both, both),
        check_vma=False,
    )
```

```python
import functools

import jax
import jax.numpy as jnp
from jax import lax
from jax.experimental import pallas as pl
from jax.experimental.pallas import tpu as pltpu
from jax.sharding import PartitionSpec as P

BF16, F32 = jnp.bfloat16, jnp.float32
VMEM = pl.BlockSpec(memory_space=pltpu.VMEM)
SMEM = pl.BlockSpec(memory_space=pltpu.SMEM)
HBM = pl.BlockSpec(memory_space=pltpu.HBM)
HIGHEST = lax.Precision.HIGHEST


def params(mib):
    return pltpu.CompilerParams(vmem_limit_bytes=mib * 2**20)


def cost(flops, moved):
    return pl.CostEstimate(flops=flops, bytes_accessed=moved, transcendentals=0)


def send_group(x, k):
    return lax.ppermute(x, "group", [(i, i ^ k) for i in range(lax.axis_size("group"))])


def send_leaf(x, k):
    return lax.ppermute(x, "leaf", [(i, i ^ k) for i in range(lax.axis_size("leaf"))])


def send_both(x, kg, kl):
    groups, leaves = lax.axis_size("group"), lax.axis_size("leaf")
    pairs = [(g * leaves + l, (g ^ kg) * leaves + (l ^ kl)) for g in range(groups) for l in range(leaves)]
    return lax.ppermute(x, ("group", "leaf"), pairs)


def gather_leaf(x, got):
    rels = [0]
    for bit in range(lax.axis_size("leaf").bit_length() - 2, 1, -1):
        if len(rels) > 1:
            got = send_leaf(x, 1 << bit)
        x = jnp.concatenate([x, got], axis=0)
        rels = rels + [r ^ (1 << bit) for r in rels]
    return [(x, rels)] + [(send_leaf(x, k), [r ^ k for r in rels]) for k in (2, 3, 1)]


def load_kernel(coupling, mass, modes, c_ref, mass_ref, m_ref, ct_ref, mt_ref, sem):
    copies = [
        pltpu.make_async_copy(src, dst, sem.at[i])
        for i, (src, dst) in enumerate(((coupling, c_ref), (modes, m_ref), (mass, mass_ref)))
    ]
    for copy in copies:
        copy.start()
    step = 512
    copies[0].wait()
    for i in range(c_ref.shape[0] // step):
        at = slice(i * step, (i + 1) * step)
        ct_ref[:, at] = c_ref[at, :].T
    copies[1].wait()
    mt_ref[...] = m_ref[...].T
    copies[2].wait()


def load_call(coupling, mass, modes):
    arrays = (coupling, mass, modes)
    shapes = [a.shape for a in arrays] + [coupling.shape[::-1], modes.shape[::-1]]
    return pl.pallas_call(
        load_kernel,
        in_specs=[HBM] * 3,
        out_specs=[VMEM] * 5,
        out_shape=[pltpu.VMEM(s, BF16) for s in shapes],
        scratch_shapes=[pltpu.SemaphoreType.DMA((3,))],
        compiler_params=params(8),
        cost_estimate=cost(0, 2 * sum(a.size for a in arrays)),
    )(*[pltpu.with_memory_space_constraint(a, pltpu.HBM) for a in arrays])


def main_kernel(n_top, low_rels, anc_top, anc_low, *refs):
    n_low = len(low_rels)
    tops, lows = refs[:n_top], refs[n_top : n_top + n_low]
    coupling, mass, modes, coef, ct = refs[n_top + n_low : n_top + n_low + 5]
    send, keep, weighted = refs[n_top + n_low + 5 : n_top + n_low + 8]
    slot_top, slot_low, stacked, shapes = refs[n_top + n_low + 8 :]
    group, leaf = lax.axis_index("group"), lax.axis_index("leaf")
    top_slots, low_slots = anc_top.shape[1], anc_low.shape[1]
    slots = top_slots + low_slots
    sr = stacked.shape[0] // (slots + 1)
    per_group = tops[0].shape[0] // sr
    rows = mass.shape[0]
    step = 512

    for b in range(slot_top.shape[0]):
        slot_top[b] = slots
    for b in range(slot_low.shape[0]):
        slot_low[b] = slots
    for j in range(top_slots):
        slot_top[anc_top[0, j]] = j
    for j in range(low_slots):
        slot_low[anc_low[0, j]] = top_slots + j
    for r, piece in enumerate(tops):
        for p in range(per_group):
            at = pl.multiple_of(slot_top[(group ^ r) * per_group + p] * sr, sr)
            stacked[pl.ds(at, sr), :] = piece[p * sr : (p + 1) * sr, :]
    for piece, rels in zip(lows, low_rels):
        for p, r in enumerate(rels):
            at = pl.multiple_of(slot_low[leaf ^ r] * sr, sr)
            stacked[pl.ds(at, sr), :] = piece[p * sr : (p + 1) * sr, :]
    send[...] = jnp.zeros(send.shape, send.dtype)
    keep[...] = jnp.zeros(keep.shape, keep.dtype)
    for i in range(rows // step):
        at = slice(i * step, (i + 1) * step)
        shapes[at, :] = (
            jnp.dot(modes[at, :], coef[...], preferred_element_type=F32)
            - jnp.dot(coupling[at, :], stacked[: slots * sr, :], preferred_element_type=F32)
        ).astype(BF16)
    for i in range(rows // step):
        at = slice(i * step, (i + 1) * step)
        weighted[at, :] = jnp.dot(mass[at, :], shapes[...], preferred_element_type=F32).astype(BF16)
    width = weighted.shape[1] // 2
    for q in range(2):
        col = pl.multiple_of(((leaf & 1) ^ q) * width, 128)
        loads = jnp.dot(ct[: top_slots * sr, :], weighted[:, pl.ds(col, width)], preferred_element_type=F32)
        for j in range(top_slots):
            b = anc_top[0, j]
            turn = (b // per_group) ^ group
            row = (turn >> 1) * per_group + ((b % per_group) ^ (((leaf >> 1) & 1) * (per_group // 2)))
            at = pl.ds(pl.multiple_of(row * sr, sr), sr)
            block = loads[j * sr : (j + 1) * sr]

            @pl.when((turn & 1) == 0)
            def _():
                keep[at, q * width : (q + 1) * width] = block

            @pl.when((turn & 1) == 1)
            def _():
                send[at, q * width : (q + 1) * width] = block.astype(BF16)


def main_call(anc_top, anc_low, tops, lows, low_rels, coupling, mass, modes, coef, ct, sr, leaves):
    rows, sw = coupling.shape
    m = coef.shape[1]
    half_rows = len(tops) * tops[0].shape[0] // 2
    top_rows = anc_top.shape[1] * sr
    flops = 2 * m * rows * (sw + rows + modes.shape[1] + top_rows)
    return pl.pallas_call(
        functools.partial(main_kernel, len(tops), low_rels),
        in_specs=[SMEM, SMEM] + [VMEM] * (len(tops) + len(lows) + 5),
        out_specs=[VMEM, VMEM, VMEM],
        out_shape=[
            jax.ShapeDtypeStruct((half_rows, m), BF16),
            jax.ShapeDtypeStruct((half_rows, m), F32),
            jax.ShapeDtypeStruct((rows, m), BF16),
        ],
        scratch_shapes=[
            pltpu.SMEM((len(tops) * tops[0].shape[0] // sr,), jnp.int32),
            pltpu.SMEM((leaves,), jnp.int32),
            pltpu.VMEM((sw + sr, m), BF16),
            pltpu.VMEM((rows, m), BF16),
        ],
        compiler_params=params(12),
        cost_estimate=cost(flops, 2 * rows * (sw + rows)),
    )(anc_top, anc_low, *tops, *lows, coupling, mass, modes, coef, ct)


def low_kernel(leaves, anc_low, ct, weighted, keep, send):
    slots = anc_low.shape[1]
    sr = keep.shape[0] * 2 // leaves
    first = ct.shape[0] - slots * sr
    bits = leaves.bit_length() - 1
    leaf = lax.axis_index("leaf")
    if slots < leaves:
        keep[...] = jnp.zeros(keep.shape, keep.dtype)
        send[...] = jnp.zeros(send.shape, send.dtype)
    part = 8
    for h in range(slots // part):
        at = slice(first + h * part * sr, first + (h + 1) * part * sr)
        loads = jnp.dot(ct[at, :], weighted[...], preferred_element_type=F32)
        for j in range(part):
            turn = anc_low[0, h * part + j] ^ leaf
            row = 0
            for i in range(1, bits):
                row += ((turn >> i) & 1) << (bits - 1 - i)
            at = pl.ds(pl.multiple_of(row * sr, sr), sr)
            block = loads[j * sr : (j + 1) * sr]

            @pl.when((turn & 1) == 0)
            def _():
                keep[at, :] = block

            @pl.when((turn & 1) == 1)
            def _():
                send[at, :] = block.astype(BF16)


def proj_kernel(mt, weighted, proj):
    proj[...] = jnp.dot(mt[...], weighted[...], preferred_element_type=F32).astype(BF16)


def proj_call(mt, weighted):
    (modes, rows), m = mt.shape, weighted.shape[1]
    return pl.pallas_call(
        proj_kernel,
        in_specs=[VMEM] * 2,
        out_specs=VMEM,
        out_shape=jax.ShapeDtypeStruct((modes, m), BF16),
        compiler_params=params(4),
        cost_estimate=cost(2 * m * rows * modes, 2 * rows * m),
    )(mt, weighted)


def low_call(anc_low, ct, weighted, sr, leaves):
    rows, m = weighted.shape
    kept = leaves // 2 * sr
    low_rows = anc_low.shape[1] * sr
    return pl.pallas_call(
        functools.partial(low_kernel, leaves),
        in_specs=[SMEM, VMEM, VMEM],
        out_specs=[VMEM] * 2,
        out_shape=[jax.ShapeDtypeStruct((kept, m), F32), jax.ShapeDtypeStruct((kept, m), BF16)],
        compiler_params=params(12),
        cost_estimate=cost(2 * m * rows * low_rows, 2 * rows * (low_rows + m)),
    )(anc_low, ct, weighted)


def part_kernel(keep, got, *outs):
    height, width = outs[0].shape
    n = 0
    for r in range(keep.shape[0] // height):
        for c in range(keep.shape[1] // width):
            at = (slice(r * height, (r + 1) * height), slice(c * width, (c + 1) * width))
            outs[n][...] = (keep[at] + got[at].astype(F32)).astype(outs[n].dtype)
            n += 1


def part_call(keep, got, high, wide):
    piece = (keep.shape[0] // high, keep.shape[1] // wide)
    return pl.pallas_call(
        part_kernel,
        in_specs=[VMEM] * 2,
        out_specs=[VMEM] * (high * wide),
        out_shape=[jax.ShapeDtypeStruct(piece, F32)] + [jax.ShapeDtypeStruct(piece, BF16)] * (high * wide - 1),
        compiler_params=params(4),
        cost_estimate=cost(keep.size, 8 * keep.size),
    )(keep, got)


def sum_kernel(keep, *refs):
    total = keep[...].astype(F32)
    for got in refs[:-1]:
        total += got[...].astype(F32)
    refs[-1][...] = total.astype(BF16)


def sum_call(keep, got):
    return pl.pallas_call(
        sum_kernel,
        in_specs=[VMEM] * (1 + len(got)),
        out_specs=VMEM,
        out_shape=jax.ShapeDtypeStruct(keep.shape, BF16),
        compiler_params=params(4),
        cost_estimate=cost(keep.size, 8 * keep.size),
    )(keep, *got)


def low_end_kernel(keep, got, kinv, out):
    total = keep[...] + got[...].astype(F32)
    out[...] = jnp.dot(kinv[...], total, preferred_element_type=F32, precision=HIGHEST)


def low_end_call(keep, got, kinv):
    return pl.pallas_call(
        low_end_kernel,
        in_specs=[VMEM] * 3,
        out_specs=VMEM,
        out_shape=jax.ShapeDtypeStruct(keep.shape, F32),
        compiler_params=params(4),
        cost_estimate=cost(12 * keep.size * 64, 8 * keep.size),
    )(keep, got, kinv)


def top_end_kernel(rels, kinv, *refs):
    parts, out, loads = refs[:-2], refs[-2], refs[-1]
    leaf = lax.axis_index("leaf")
    sr = kinv.shape[1]
    for part, r in zip(parts, rels):
        height, width = part.shape
        there = leaf ^ r
        row = pl.multiple_of(((there >> 1) & 1) * height, height)
        col = pl.multiple_of((there & 1) * width, 128)
        loads[pl.ds(row, height), pl.ds(col, width)] = part[...]
    for b in range(out.shape[0] // sr):
        at = slice(b * sr, (b + 1) * sr)
        block = kinv[at, :]
        coarse = block.astype(BF16)
        fine = (block - coarse.astype(F32)).astype(BF16)
        rest = (block - coarse.astype(F32) - fine.astype(F32)).astype(BF16)
        parts = jnp.concatenate([coarse, fine, rest], axis=0)
        product = jnp.dot(parts, loads[at, :], preferred_element_type=F32)
        out[at, :] = product[:sr] + product[sr : 2 * sr] + product[2 * sr :]


def top_end_call(parts, rels, kinv, m):
    rows = kinv.shape[0]
    return pl.pallas_call(
        functools.partial(top_end_kernel, rels),
        in_specs=[VMEM] * (1 + len(parts)),
        out_specs=VMEM,
        out_shape=jax.ShapeDtypeStruct((rows, m), F32),
        scratch_shapes=[pltpu.VMEM((rows, m), BF16)],
        compiler_params=params(8),
        cost_estimate=cost(12 * rows * m * 64, 8 * rows * m),
    )(kinv, *parts)


def per_device(
    top_modes, low_modes, anc_top, anc_low, coupling, leaf_mass, leaf_modes, leaf_coef, kinv_top, kinv_low
):
    sr = kinv_low.shape[1]
    m = low_modes.shape[1]
    leaves = lax.axis_size("leaf")
    far_low = send_leaf(low_modes, leaves // 2)
    far_top = send_group(top_modes, 2)
    loaded = load_call(coupling, leaf_mass, leaf_modes)
    far_low, far_top, *loaded = lax.optimization_barrier((far_low, far_top, *loaded))
    coupling, leaf_mass, leaf_modes, ct, mt = loaded
    held = gather_leaf(low_modes, far_low)
    tops = [top_modes, send_group(top_modes, 1), far_top, send_group(far_top, 1)]
    send, keep, weighted = main_call(
        anc_top,
        anc_low,
        tops,
        [a for a, _ in held],
        [r for _, r in held],
        coupling,
        leaf_mass,
        leaf_modes,
        leaf_coef,
        ct,
        sr,
        leaves,
    )
    got = send_group(send, 1)
    low_keep, low_send = low_call(anc_low, ct, weighted, sr, leaves)
    low_keep, low_send, got = lax.optimization_barrier((low_keep, low_send, got))
    low_got = send_leaf(low_send, 1)
    keep, send = part_call(keep, got, 2, 1)
    got = send_group(send, 2)
    keep, *sends = part_call(keep, got, 2, 2)
    weighted, keep = lax.optimization_barrier((weighted, keep))
    got = [send_leaf(x, k) for x, k in zip(sends, (1, 2, 3))]
    leaf_proj = proj_call(mt, weighted)
    low_keep, got[1] = lax.optimization_barrier((low_keep, got[1]))
    low_keep, low_send = part_call(low_keep, low_got, 2, 1)
    low_got = send_leaf(low_send, 2)
    total = sum_call(keep, got)
    low_keep, total = lax.optimization_barrier((low_keep, total))
    for bit in range(2, leaves.bit_length() - 1):
        low_keep, low_send = part_call(low_keep, low_got, 2, 1)
        low_got = send_leaf(low_send, 1 << bit)
        total = sum_call(total, [send_leaf(total, 1 << bit)])
    rels = (0, 2, 1, 3)
    parts = [total] + [send_leaf(total, r) for r in rels[1:]]
    new_low = low_end_call(low_keep, low_got, kinv_low)
    new_top = top_end_call(parts, rels, kinv_top, m)
    return (new_top, new_low, leaf_proj)


def solution(mesh):
    both = P(("group", "leaf"), None)
    return jax.shard_map(
        per_device,
        mesh=mesh,
        in_specs=(P("group", None), both, both, both, both, both, both, both, P("group", None), both),
        out_specs=(P("group", None), both, both),
        check_vma=False,
    )
```

```python
import functools

import jax
import jax.numpy as jnp
from jax import lax
from jax.experimental import pallas as pl
from jax.experimental.pallas import tpu as pltpu
from jax.sharding import PartitionSpec as P

BF16, F32 = jnp.bfloat16, jnp.float32
VMEM = pl.BlockSpec(memory_space=pltpu.VMEM)
SMEM = pl.BlockSpec(memory_space=pltpu.SMEM)
HBM = pl.BlockSpec(memory_space=pltpu.HBM)
FILL = 20_000_000_000


def params(mib):
    return pltpu.CompilerParams(vmem_limit_bytes=mib * 2**20)


def cost(flops, moved):
    return pl.CostEstimate(flops=flops, bytes_accessed=moved, transcendentals=0)


def send_group(x, k):
    return lax.ppermute(x, "group", [(i, i ^ k) for i in range(lax.axis_size("group"))])


def send_leaf(x, k):
    return lax.ppermute(x, "leaf", [(i, i ^ k) for i in range(lax.axis_size("leaf"))])


def send_by_core(x, even, odd):
    groups, leaves = lax.axis_size("group"), lax.axis_size("leaf")
    pairs = []
    for g in range(groups):
        far, near = odd if g & 1 else even
        pairs += [(g * leaves + l, (g ^ far) * leaves + (l ^ near)) for l in range(leaves)]
    return lax.ppermute(x, ("group", "leaf"), pairs)


def gather_leaf(x, got):
    rels = [0]
    for bit in range(lax.axis_size("leaf").bit_length() - 2, 1, -1):
        if len(rels) > 1:
            got = send_leaf(x, 1 << bit)
        x = jnp.concatenate([x, got], axis=0)
        rels = rels + [r ^ (1 << bit) for r in rels]
    return [(x, rels)] + [(send_leaf(x, k), [r ^ k for r in rels]) for k in (2, 3, 1)]


def load_kernel(turned, *refs):
    n = len(turned)
    sources, copies, turns, sem = refs[:n], refs[n : 2 * n], list(refs[2 * n : -1]), refs[-1]
    moves = [pltpu.make_async_copy(s, d, sem.at[i]) for i, (s, d) in enumerate(zip(sources, copies))]
    for move in moves:
        move.start()
    for move, copy, turn in zip(moves, copies, turned):
        move.wait()
        if turn:
            out = turns.pop(0)
            step = 512
            for i in range(copy.shape[0] // step):
                at = slice(i * step, (i + 1) * step)
                out[:, at] = copy[at, :].T


def load_call(arrays, turned):
    shapes = [a.shape for a in arrays] + [a.shape[::-1] for a, t in zip(arrays, turned) if t]
    return pl.pallas_call(
        functools.partial(load_kernel, turned),
        in_specs=[HBM] * len(arrays),
        out_specs=[VMEM] * len(shapes),
        out_shape=[pltpu.VMEM(s, BF16) for s in shapes],
        scratch_shapes=[pltpu.SemaphoreType.DMA((len(arrays),))],
        compiler_params=params(8),
        cost_estimate=cost(FILL, 2 * sum(a.size for a in arrays)),
    )(*[pltpu.with_memory_space_constraint(a, pltpu.HBM) for a in arrays])


def main_kernel(n_top, low_rels, anc_top, anc_low, *refs):
    n_low = len(low_rels)
    tops, lows = refs[:n_top], refs[n_top : n_top + n_low]
    coupling, mass, modes, coef, ct = refs[n_top + n_low : n_top + n_low + 5]
    send, keep, weighted = refs[n_top + n_low + 5 : n_top + n_low + 8]
    slot_top, slot_low, stacked, shapes, loads = refs[n_top + n_low + 8 :]
    group, leaf = lax.axis_index("group"), lax.axis_index("leaf")
    top_slots, low_slots = anc_top.shape[1], anc_low.shape[1]
    slots = top_slots + low_slots
    sr = stacked.shape[0] // (slots + 1)
    per_group = tops[0].shape[0] // sr
    rows = mass.shape[0]
    step = 512

    for b in range(slot_top.shape[0]):
        slot_top[b] = slots
    for b in range(slot_low.shape[0]):
        slot_low[b] = slots
    for j in range(top_slots):
        slot_top[anc_top[0, j]] = j
    for j in range(low_slots):
        slot_low[anc_low[0, j]] = top_slots + j
    for r, piece in enumerate(tops):
        for p in range(per_group):
            at = pl.multiple_of(slot_top[(group ^ r) * per_group + p] * sr, sr)
            stacked[pl.ds(at, sr), :] = piece[p * sr : (p + 1) * sr, :]
    for piece, rels in zip(lows, low_rels):
        for p, r in enumerate(rels):
            at = pl.multiple_of(slot_low[leaf ^ r] * sr, sr)
            stacked[pl.ds(at, sr), :] = piece[p * sr : (p + 1) * sr, :]
    for i in range(rows // step):
        at = slice(i * step, (i + 1) * step)
        shapes[at, :] = (
            jnp.dot(modes[at, :], coef[...], preferred_element_type=F32)
            - jnp.dot(coupling[at, :], stacked[: slots * sr, :], preferred_element_type=F32)
        ).astype(BF16)
    for i in range(rows // step):
        at = slice(i * step, (i + 1) * step)
        weighted[at, :] = jnp.dot(mass[at, :], shapes[...], preferred_element_type=F32).astype(BF16)
    width = weighted.shape[1] // 2
    core, near, high = group & 1, leaf & 1, (leaf >> 1) & 1
    top_rows = top_slots * sr
    for q in range(2):
        loads[q, :top_rows, :] = jnp.dot(
            ct[:top_rows, :], weighted[:, q * width : (q + 1) * width], preferred_element_type=F32
        )
        loads[q, top_rows:, :] = jnp.zeros((sr, width), F32)
    for out, owner in ((keep, core), (send, 1 - core)):
        for first in range(2):
            for second in range(2):
                far = jnp.where(owner == 0, first, second) ^ (group >> 1)
                q = jnp.where(owner == 0, second, first) ^ near
                for p in range(per_group):
                    block = (2 * far + owner) * per_group + (p ^ (high * (per_group // 2)))
                    slot = jnp.minimum(slot_top[block], top_slots)
                    at = pl.ds(pl.multiple_of(slot * sr, sr), sr)
                    to = ((2 * first + second) * per_group + p) * sr
                    out[to : to + sr, :] = loads[q, at, :].astype(out.dtype)


def main_call(anc_top, anc_low, tops, lows, low_rels, coupling, mass, modes, coef, ct, sr, leaves):
    rows, sw = coupling.shape
    m = coef.shape[1]
    half_rows = len(tops) * tops[0].shape[0] // 2
    top_rows = anc_top.shape[1] * sr
    flops = 2 * m * rows * (sw + rows + modes.shape[1] + top_rows)
    return pl.pallas_call(
        functools.partial(main_kernel, len(tops), low_rels),
        in_specs=[SMEM, SMEM] + [VMEM] * (len(tops) + len(lows) + 5),
        out_specs=[VMEM, VMEM, VMEM],
        out_shape=[
            jax.ShapeDtypeStruct((2 * half_rows, m // 2), BF16),
            jax.ShapeDtypeStruct((2 * half_rows, m // 2), F32),
            jax.ShapeDtypeStruct((rows, m), BF16),
        ],
        scratch_shapes=[
            pltpu.SMEM((len(tops) * tops[0].shape[0] // sr,), jnp.int32),
            pltpu.SMEM((leaves,), jnp.int32),
            pltpu.VMEM((sw + sr, m), BF16),
            pltpu.VMEM((rows, m), BF16),
            pltpu.VMEM((2, top_rows + sr, m // 2), F32),
        ],
        compiler_params=params(12),
        cost_estimate=cost(flops, 2 * rows * (sw + rows)),
    )(anc_top, anc_low, *tops, *lows, coupling, mass, modes, coef, ct)


def low_kernel(leaves, anc_low, ct, weighted, keep, send, slot_low, loads):
    slots = anc_low.shape[1]
    sr = keep.shape[0] * 2 // leaves
    start = ct.shape[0] - slots * sr
    bits = leaves.bit_length() - 1
    leaf = lax.axis_index("leaf")
    even = (lax.axis_index("group") & 1) == 0
    for k in range(leaves):
        slot_low[k] = slots
    for j in range(slots):
        slot_low[anc_low[0, j]] = j
    loads[: slots * sr, :] = jnp.dot(ct[start:, :], weighted[...], preferred_element_type=F32)
    loads[slots * sr :, :] = jnp.zeros((sr, loads.shape[1]), F32)
    for first, out in enumerate((keep, send)):
        for row in range(leaves // 2):
            second = row >> (bits - 2)
            turn = jnp.where(even, 2 * first + second, 2 * second + first)
            for i in range(2, bits):
                turn += ((row >> (bits - 1 - i)) & 1) << i
            at = pl.ds(pl.multiple_of(slot_low[leaf ^ turn] * sr, sr), sr)
            out[row * sr : (row + 1) * sr, :] = loads[at, :].astype(out.dtype)


def proj_kernel(mt, weighted, proj):
    proj[...] = jnp.dot(mt[...], weighted[...], preferred_element_type=F32).astype(BF16)


def proj_call(mt, weighted):
    (modes, rows), m = mt.shape, weighted.shape[1]
    return pl.pallas_call(
        proj_kernel,
        in_specs=[VMEM] * 2,
        out_specs=VMEM,
        out_shape=jax.ShapeDtypeStruct((modes, m), BF16),
        compiler_params=params(4),
        cost_estimate=cost(FILL, 2 * rows * m),
    )(mt, weighted)


def low_call(anc_low, ct, weighted, sr, leaves):
    rows, m = weighted.shape
    kept = leaves // 2 * sr
    low_rows = anc_low.shape[1] * sr
    return pl.pallas_call(
        functools.partial(low_kernel, leaves),
        in_specs=[SMEM, VMEM, VMEM],
        out_specs=[VMEM] * 2,
        out_shape=[jax.ShapeDtypeStruct((kept, m), F32), jax.ShapeDtypeStruct((kept, m), BF16)],
        scratch_shapes=[pltpu.SMEM((leaves,), jnp.int32), pltpu.VMEM((low_rows + sr, m), F32)],
        compiler_params=params(12),
        cost_estimate=cost(2 * m * rows * low_rows, 2 * rows * (low_rows + m)),
    )(anc_low, ct, weighted)


def part_kernel(n_got, keep, *refs):
    got, outs = refs[:n_got], refs[n_got:]
    height, width = outs[0].shape
    n = 0
    for r in range(keep.shape[0] // height):
        for c in range(keep.shape[1] // width):
            at = (slice(r * height, (r + 1) * height), slice(c * width, (c + 1) * width))
            total = keep[at]
            for g in got:
                total += g[at].astype(F32)
            outs[n][...] = total.astype(outs[n].dtype)
            n += 1


def part_call(keep, got, high, wide):
    piece = (keep.shape[0] // high, keep.shape[1] // wide)
    return pl.pallas_call(
        functools.partial(part_kernel, len(got)),
        in_specs=[VMEM] * (1 + len(got)),
        out_specs=[VMEM] * (high * wide),
        out_shape=[jax.ShapeDtypeStruct(piece, F32)] + [jax.ShapeDtypeStruct(piece, BF16)] * (high * wide - 1),
        compiler_params=params(4),
        cost_estimate=cost(keep.size, 8 * keep.size),
    )(keep, *got)


def sum_kernel(keep, *refs):
    total = keep[...].astype(F32)
    for got in refs[:-1]:
        total += got[...].astype(F32)
    refs[-1][...] = total.astype(BF16)


def sum_call(keep, got):
    return pl.pallas_call(
        sum_kernel,
        in_specs=[VMEM] * (1 + len(got)),
        out_specs=VMEM,
        out_shape=jax.ShapeDtypeStruct(keep.shape, BF16),
        compiler_params=params(4),
        cost_estimate=cost(keep.size, 8 * keep.size),
    )(keep, *got)


def solve(kinv, loads):
    def parts(x):
        coarse = x.astype(BF16)
        fine = (x - coarse.astype(F32)).astype(BF16)
        return coarse, fine, (x - coarse.astype(F32) - fine.astype(F32)).astype(BF16)

    n = kinv.shape[0]
    total = None
    for i, part in enumerate(parts(loads) if loads.dtype == F32 else (loads,)):
        left = jnp.concatenate(parts(kinv)[: 3 - i], axis=0)
        product = jnp.dot(left, part, preferred_element_type=F32)
        for k in range(3 - i):
            term = product[k * n : (k + 1) * n]
            total = term if total is None else total + term
    return total


def low_end_kernel(kinv, keep, got, out):
    out[...] = solve(kinv[...], keep[...] + got[...].astype(F32))


def low_end_call(kinv, keep, got):
    return pl.pallas_call(
        low_end_kernel,
        in_specs=[VMEM] * 3,
        out_specs=VMEM,
        out_shape=jax.ShapeDtypeStruct(keep.shape, F32),
        compiler_params=params(4),
        cost_estimate=cost(12 * keep.size * 64, 8 * keep.size),
    )(kinv, keep, got)


def top_end_kernel(rels, kinv, *refs):
    parts, out, loads = refs[:-2], refs[-2], refs[-1]
    leaf = lax.axis_index("leaf")
    even = (lax.axis_index("group") & 1) == 0
    sr = kinv.shape[1]
    for part, (r_even, r_odd) in zip(parts, rels):
        height, width = part.shape
        there = leaf ^ jnp.where(even, r_even, r_odd)
        row = pl.multiple_of(((there >> 1) & 1) * height, height)
        col = pl.multiple_of((there & 1) * width, 128)
        loads[pl.ds(row, height), pl.ds(col, width)] = part[...]
    for b in range(out.shape[0] // sr):
        at = slice(b * sr, (b + 1) * sr)
        out[at, :] = solve(kinv[at, :], loads[at, :])


def top_end_call(parts, rels, kinv, m):
    rows = kinv.shape[0]
    return pl.pallas_call(
        functools.partial(top_end_kernel, rels),
        in_specs=[VMEM] * (1 + len(parts)),
        out_specs=VMEM,
        out_shape=jax.ShapeDtypeStruct((rows, m), F32),
        scratch_shapes=[pltpu.VMEM((rows, m), BF16)],
        compiler_params=params(8),
        cost_estimate=cost(12 * rows * m * 64, 8 * rows * m),
    )(kinv, *parts)


def per_device(
    top_modes, low_modes, anc_top, anc_low, coupling, leaf_mass, leaf_modes, leaf_coef, kinv_top, kinv_low
):
    sr = kinv_low.shape[1]
    m = low_modes.shape[1]
    leaves = lax.axis_size("leaf")
    near_top = send_group(top_modes, 1)
    far_low = send_leaf(low_modes, leaves // 2)
    near_top, to_send = lax.optimization_barrier((near_top, top_modes))
    far_top = send_group(to_send, 2)
    leaf_modes, mt = load_call((leaf_modes,), (True,))
    far_low, mt = lax.optimization_barrier((far_low, mt))
    held = gather_leaf(low_modes, far_low)
    coupling, leaf_mass, ct = load_call((coupling, leaf_mass), (True, False))
    tops = [top_modes, near_top, far_top, send_group(far_top, 1)]
    send, keep, weighted = main_call(
        anc_top,
        anc_low,
        tops,
        [a for a, _ in held],
        [r for _, r in held],
        coupling,
        leaf_mass,
        leaf_modes,
        leaf_coef,
        ct,
        sr,
        leaves,
    )
    got = send_group(send, 1)
    low_keep, low_send = low_call(anc_low, ct, weighted, sr, leaves)
    low_keep, low_send, got = lax.optimization_barrier((low_keep, low_send, got))
    low_got = send_by_core(low_send, (0, 2), (0, 1))
    keep, send = part_call(keep, [got], 2, 1)
    send, weighted = lax.optimization_barrier((send, weighted))
    got = send_by_core(send, (2, 0), (0, 1))
    leaf_proj = proj_call(mt, weighted)
    got, leaf_proj = lax.optimization_barrier((got, leaf_proj))
    keep, *sends = part_call(keep, [got], 4, 1)
    got = [
        send_by_core(x, *there)
        for x, there in zip(sends, (((0, 2), (0, 2)), ((0, 1), (2, 0)), ((0, 3), (2, 2))))
    ]
    low_keep, got[1] = lax.optimization_barrier((low_keep, got[1]))
    low_keep, low_send = part_call(low_keep, [low_got], 2, 1)
    low_got = send_by_core(low_send, (0, 1), (0, 2))
    total = sum_call(keep, got)
    low_keep, total = lax.optimization_barrier((low_keep, total))
    for bit in range(2, leaves.bit_length() - 1):
        low_keep, low_send = part_call(low_keep, [low_got], 2, 1)
        low_got = send_leaf(low_send, 1 << bit)
        total = sum_call(total, [send_leaf(total, 1 << bit)])
    rels = ((0, 0), (1, 2), (2, 1), (3, 3))
    parts = [total] + [send_by_core(total, (0, even), (0, odd)) for even, odd in rels[1:]]
    new_low = low_end_call(kinv_low, low_keep, low_got)
    new_top = top_end_call(parts, rels, kinv_top, m)
    return (new_top, new_low, leaf_proj)


def solution(mesh):
    both = P(("group", "leaf"), None)
    return jax.shard_map(
        per_device,
        mesh=mesh,
        in_specs=(P("group", None), both, both, both, both, both, both, both, P("group", None), both),
        out_specs=(P("group", None), both, both),
        check_vma=False,
    )
```

```python
import functools

import jax
import jax.numpy as jnp
from jax import lax
from jax.experimental import pallas as pl
from jax.experimental.pallas import tpu as pltpu
from jax.sharding import PartitionSpec as P

BF16, F32 = jnp.bfloat16, jnp.float32
VMEM = pl.BlockSpec(memory_space=pltpu.VMEM)
SMEM = pl.BlockSpec(memory_space=pltpu.SMEM)
HBM = pl.BlockSpec(memory_space=pltpu.HBM)
FILL = 20_000_000_000


def params(mib):
    return pltpu.CompilerParams(vmem_limit_bytes=mib * 2**20)


def cost(flops, moved):
    return pl.CostEstimate(flops=flops, bytes_accessed=moved, transcendentals=0)


def send_group(x, k):
    return lax.ppermute(x, "group", [(i, i ^ k) for i in range(lax.axis_size("group"))])


def send_leaf(x, k):
    return lax.ppermute(x, "leaf", [(i, i ^ k) for i in range(lax.axis_size("leaf"))])


def send_by_core(x, even, odd):
    groups, leaves = lax.axis_size("group"), lax.axis_size("leaf")
    pairs = []
    for g in range(groups):
        far, near = odd if g & 1 else even
        pairs += [(g * leaves + l, (g ^ far) * leaves + (l ^ near)) for l in range(leaves)]
    return lax.ppermute(x, ("group", "leaf"), pairs)


def gather_leaf(x, got):
    rels = [0]
    for bit in range(lax.axis_size("leaf").bit_length() - 2, 1, -1):
        if len(rels) > 1:
            got = send_leaf(x, 1 << bit)
        x = jnp.concatenate([x, got], axis=0)
        rels = rels + [r ^ (1 << bit) for r in rels]
    return [(x, rels, rels)] + [(send_by_core(x, (0, a), (0, b)), [r ^ a for r in rels], [r ^ b for r in rels]) for a, b in ((3, 3), (2, 1), (1, 2))]


def load_kernel(turned, step, *refs):
    n = len(turned)
    sources, copies, turns, sem = refs[:n], refs[n : 2 * n], list(refs[2 * n : -1]), refs[-1]
    pieces = []
    for source, copy, turn in zip(sources, copies, turned):
        out = turns.pop(0) if turn else None
        for i in range(source.shape[0] // step):
            at = slice(i * step, (i + 1) * step)
            move = pltpu.make_async_copy(source.at[at, :], copy.at[at, :], sem.at[len(pieces)])
            move.start()
            pieces.append((move, copy, at, out))
    for move, copy, at, out in pieces:
        move.wait()
        if out is not None:
            out[:, at] = copy[at, :].T


def load_call(arrays, turned):
    shapes = [a.shape for a in arrays] + [a.shape[::-1] for a, t in zip(arrays, turned) if t]
    step = 512
    return pl.pallas_call(
        functools.partial(load_kernel, turned, step),
        in_specs=[HBM] * len(arrays),
        out_specs=[VMEM] * len(shapes),
        out_shape=[pltpu.VMEM(s, BF16) for s in shapes],
        scratch_shapes=[pltpu.SemaphoreType.DMA((sum(a.shape[0] // step for a in arrays),))],
        compiler_params=params(8),
        cost_estimate=cost(FILL, 2 * sum(a.size for a in arrays)),
    )(*[pltpu.with_memory_space_constraint(a, pltpu.HBM) for a in arrays])


def fill_slots(slot_of, anc):
    for b in range(slot_of.shape[0]):
        slot_of[b] = anc.shape[1]
    for j in range(anc.shape[1]):
        slot_of[anc[0, j]] = j


def first_kernel(n_top, anc_top, *refs):
    tops = refs[:n_top]
    coupling, modes, coef, part, slot_top, stacked = refs[n_top:]
    group = lax.axis_index("group")
    slots = anc_top.shape[1]
    sr = stacked.shape[0] // (slots + 1)
    per_group = tops[0].shape[0] // sr
    fill_slots(slot_top, anc_top)
    for r, piece in enumerate(tops):
        for p in range(per_group):
            at = pl.multiple_of(slot_top[(group ^ r) * per_group + p] * sr, sr)
            stacked[pl.ds(at, sr), :] = piece[p * sr : (p + 1) * sr, :]
    step = 512
    for i in range(part.shape[0] // step):
        at = slice(i * step, (i + 1) * step)
        part[at, :] = jnp.dot(modes[at, :], coef[...], preferred_element_type=F32) - jnp.dot(
            coupling[at, : slots * sr], stacked[: slots * sr, :], preferred_element_type=F32
        )


def first_call(anc_top, tops, coupling, modes, coef, sr):
    rows, m = coupling.shape[0], coef.shape[1]
    top_rows = anc_top.shape[1] * sr
    return pl.pallas_call(
        functools.partial(first_kernel, len(tops)),
        in_specs=[SMEM] + [VMEM] * (len(tops) + 3),
        out_specs=VMEM,
        out_shape=jax.ShapeDtypeStruct((rows, m), F32),
        scratch_shapes=[
            pltpu.SMEM((len(tops) * tops[0].shape[0] // sr,), jnp.int32),
            pltpu.VMEM((top_rows + sr, m), BF16),
        ],
        compiler_params=params(8),
        cost_estimate=cost(0, 0),
    )(anc_top, *tops, coupling, modes, coef)


def main_kernel(per_group, low_rels, anc_top, anc_low, *refs):
    n_low = len(low_rels)
    lows = refs[:n_low]
    part, coupling, mass, ct, send, keep, weighted = refs[n_low : n_low + 7]
    slot_top, slot_low, stacked, shapes, loads = refs[n_low + 7 :]
    group, leaf = lax.axis_index("group"), lax.axis_index("leaf")
    top_slots, low_slots = anc_top.shape[1], anc_low.shape[1]
    sr = stacked.shape[0] // (low_slots + 1)
    top_rows = top_slots * sr
    rows = mass.shape[0]
    step = 512

    fill_slots(slot_top, anc_top)
    fill_slots(slot_low, anc_low)
    even = (group & 1) == 0
    for piece, rels in zip(lows, low_rels):
        for p, (r_even, r_odd) in enumerate(zip(*rels)):
            at = pl.multiple_of(slot_low[leaf ^ jnp.where(even, r_even, r_odd)] * sr, sr)
            stacked[pl.ds(at, sr), :] = piece[p * sr : (p + 1) * sr, :]
    for i in range(rows // step):
        at = slice(i * step, (i + 1) * step)
        shapes[at, :] = (
            part[at, :]
            - jnp.dot(coupling[at, top_rows:], stacked[: low_slots * sr, :], preferred_element_type=F32)
        ).astype(BF16)
    for i in range(rows // step):
        at = slice(i * step, (i + 1) * step)
        weighted[at, :] = jnp.dot(mass[at, :], shapes[...], preferred_element_type=F32).astype(BF16)
    width = weighted.shape[1] // 2
    core, near, high = group & 1, leaf & 1, (leaf >> 1) & 1
    for q in range(2):
        loads[q, :top_rows, :] = jnp.dot(
            ct[:top_rows, :], weighted[:, q * width : (q + 1) * width], preferred_element_type=F32
        )
        loads[q, top_rows:, :] = jnp.zeros((sr, width), F32)
    for out, owner in ((keep, core), (send, 1 - core)):
        for first in range(2):
            for second in range(2):
                far = jnp.where(owner == 0, first, second) ^ (group >> 1)
                q = jnp.where(owner == 0, second, first) ^ near
                for p in range(per_group):
                    block = (2 * far + owner) * per_group + (p ^ (high * (per_group // 2)))
                    at = pl.ds(pl.multiple_of(slot_top[block] * sr, sr), sr)
                    to = ((2 * first + second) * per_group + p) * sr
                    out[to : to + sr, :] = loads[q, at, :].astype(out.dtype)


def main_call(anc_top, anc_low, part, lows, low_rels, coupling, mass, ct, sr, leaves, groups, per_group):
    rows, m = part.shape
    half_rows = groups * per_group * sr // 2
    top_rows, low_rows = anc_top.shape[1] * sr, anc_low.shape[1] * sr
    flops = 2 * m * rows * (low_rows + rows + top_rows)
    return pl.pallas_call(
        functools.partial(main_kernel, per_group, low_rels),
        in_specs=[SMEM, SMEM] + [VMEM] * (len(lows) + 4),
        out_specs=[VMEM, VMEM, VMEM],
        out_shape=[
            jax.ShapeDtypeStruct((2 * half_rows, m // 2), BF16),
            jax.ShapeDtypeStruct((2 * half_rows, m // 2), F32),
            jax.ShapeDtypeStruct((rows, m), BF16),
        ],
        scratch_shapes=[
            pltpu.SMEM((groups * per_group,), jnp.int32),
            pltpu.SMEM((leaves,), jnp.int32),
            pltpu.VMEM((low_rows + sr, m), BF16),
            pltpu.VMEM((rows, m), BF16),
            pltpu.VMEM((2, top_rows + sr, m // 2), F32),
        ],
        compiler_params=params(12),
        cost_estimate=cost(flops, 2 * rows * (low_rows + rows)),
    )(anc_top, anc_low, *lows, part, coupling, mass, ct)


def low_kernel(leaves, anc_low, ct, weighted, keep, send, slot_low, loads):
    slots = anc_low.shape[1]
    sr = keep.shape[0] * 2 // leaves
    start = ct.shape[0] - slots * sr
    bits = leaves.bit_length() - 1
    leaf = lax.axis_index("leaf")
    even = (lax.axis_index("group") & 1) == 0
    fill_slots(slot_low, anc_low)
    loads[: slots * sr, :] = jnp.dot(ct[start:, :], weighted[...], preferred_element_type=F32)
    loads[slots * sr :, :] = jnp.zeros((sr, loads.shape[1]), F32)
    for first, out in enumerate((keep, send)):
        for row in range(leaves // 2):
            second = row >> (bits - 2)
            turn = jnp.where(even, 2 * first + second, 2 * second + first)
            for i in range(2, bits):
                turn += ((row >> (bits - 1 - i)) & 1) << i
            at = pl.ds(pl.multiple_of(slot_low[leaf ^ turn] * sr, sr), sr)
            out[row * sr : (row + 1) * sr, :] = loads[at, :].astype(out.dtype)


def proj_kernel(mt, weighted, proj):
    proj[...] = jnp.dot(mt[...], weighted[...], preferred_element_type=F32).astype(BF16)


def proj_call(mt, weighted):
    (modes, rows), m = mt.shape, weighted.shape[1]
    return pl.pallas_call(
        proj_kernel,
        in_specs=[VMEM] * 2,
        out_specs=VMEM,
        out_shape=jax.ShapeDtypeStruct((modes, m), BF16),
        compiler_params=params(4),
        cost_estimate=cost(FILL, 2 * rows * m),
    )(mt, weighted)


def low_call(anc_low, ct, weighted, sr, leaves):
    rows, m = weighted.shape
    kept = leaves // 2 * sr
    low_rows = anc_low.shape[1] * sr
    return pl.pallas_call(
        functools.partial(low_kernel, leaves),
        in_specs=[SMEM, VMEM, VMEM],
        out_specs=[VMEM] * 2,
        out_shape=[jax.ShapeDtypeStruct((kept, m), F32), jax.ShapeDtypeStruct((kept, m), BF16)],
        scratch_shapes=[pltpu.SMEM((leaves,), jnp.int32), pltpu.VMEM((low_rows + sr, m), F32)],
        compiler_params=params(12),
        cost_estimate=cost(2 * m * rows * low_rows, 2 * rows * (low_rows + m)),
    )(anc_low, ct, weighted)


def part_kernel(n_got, keep, *refs):
    got, outs = refs[:n_got], refs[n_got:]
    height, width = outs[0].shape
    n = 0
    for r in range(keep.shape[0] // height):
        for c in range(keep.shape[1] // width):
            at = (slice(r * height, (r + 1) * height), slice(c * width, (c + 1) * width))
            total = keep[at]
            for g in got:
                total += g[at].astype(F32)
            outs[n][...] = total.astype(outs[n].dtype)
            n += 1


def part_call(keep, got, high, wide):
    piece = (keep.shape[0] // high, keep.shape[1] // wide)
    return pl.pallas_call(
        functools.partial(part_kernel, len(got)),
        in_specs=[VMEM] * (1 + len(got)),
        out_specs=[VMEM] * (high * wide),
        out_shape=[jax.ShapeDtypeStruct(piece, F32)] + [jax.ShapeDtypeStruct(piece, BF16)] * (high * wide - 1),
        compiler_params=params(4),
        cost_estimate=cost(keep.size, 8 * keep.size),
    )(keep, *got)


def sum_kernel(keep, *refs):
    total = keep[...].astype(F32)
    for got in refs[:-1]:
        total += got[...].astype(F32)
    refs[-1][...] = total.astype(BF16)


def sum_call(keep, got):
    return pl.pallas_call(
        sum_kernel,
        in_specs=[VMEM] * (1 + len(got)),
        out_specs=VMEM,
        out_shape=jax.ShapeDtypeStruct(keep.shape, BF16),
        compiler_params=params(4),
        cost_estimate=cost(keep.size, 8 * keep.size),
    )(keep, *got)


def solve(kinv, loads):
    def parts(x):
        coarse = x.astype(BF16)
        fine = (x - coarse.astype(F32)).astype(BF16)
        return coarse, fine, (x - coarse.astype(F32) - fine.astype(F32)).astype(BF16)

    n = kinv.shape[0]
    total = None
    for i, part in enumerate(parts(loads) if loads.dtype == F32 else (loads,)):
        left = jnp.concatenate(parts(kinv)[: 3 - i], axis=0)
        product = jnp.dot(left, part, preferred_element_type=F32)
        for k in range(3 - i):
            term = product[k * n : (k + 1) * n]
            total = term if total is None else total + term
    return total


def low_end_kernel(kinv, keep, got, out):
    out[...] = solve(kinv[...], keep[...] + got[...].astype(F32))


def low_end_call(kinv, keep, got):
    return pl.pallas_call(
        low_end_kernel,
        in_specs=[VMEM] * 3,
        out_specs=VMEM,
        out_shape=jax.ShapeDtypeStruct(keep.shape, F32),
        compiler_params=params(4),
        cost_estimate=cost(12 * keep.size * 64, 8 * keep.size),
    )(kinv, keep, got)


def top_end_kernel(rels, kinv, *refs):
    parts, out, loads = refs[:-2], refs[-2], refs[-1]
    leaf = lax.axis_index("leaf")
    even = (lax.axis_index("group") & 1) == 0
    sr = kinv.shape[1]
    for part, (r_even, r_odd) in zip(parts, rels):
        height, width = part.shape
        there = leaf ^ jnp.where(even, r_even, r_odd)
        row = pl.multiple_of(((there >> 1) & 1) * height, height)
        col = pl.multiple_of((there & 1) * width, 128)
        loads[pl.ds(row, height), pl.ds(col, width)] = part[...]
    for b in range(out.shape[0] // sr):
        at = slice(b * sr, (b + 1) * sr)
        out[at, :] = solve(kinv[at, :], loads[at, :])


def top_end_call(parts, rels, kinv, m):
    rows = kinv.shape[0]
    return pl.pallas_call(
        functools.partial(top_end_kernel, rels),
        in_specs=[VMEM] * (1 + len(parts)),
        out_specs=VMEM,
        out_shape=jax.ShapeDtypeStruct((rows, m), F32),
        scratch_shapes=[pltpu.VMEM((rows, m), BF16)],
        compiler_params=params(8),
        cost_estimate=cost(12 * rows * m * 64, 8 * rows * m),
    )(kinv, *parts)


def per_device(
    top_modes, low_modes, anc_top, anc_low, coupling, leaf_mass, leaf_modes, leaf_coef, kinv_top, kinv_low
):
    sr = kinv_low.shape[1]
    m = low_modes.shape[1]
    leaves = lax.axis_size("leaf")
    near_top = send_group(top_modes, 1)
    far_low = send_leaf(low_modes, leaves // 2)
    near_top, to_send = lax.optimization_barrier((near_top, top_modes))
    far_top = send_group(to_send, 2)
    coupling, leaf_modes, ct, mt = load_call((coupling, leaf_modes), (True, True))
    far_low, ct = lax.optimization_barrier((far_low, ct))
    held = gather_leaf(low_modes, far_low)
    (leaf_mass,) = load_call((leaf_mass,), (False,))
    tops = [top_modes, near_top, far_top, send_group(far_top, 1)]
    part = first_call(anc_top, tops, coupling, leaf_modes, leaf_coef, sr)
    send, keep, weighted = main_call(
        anc_top,
        anc_low,
        part,
        [h[0] for h in held],
        [h[1:] for h in held],
        coupling,
        leaf_mass,
        ct,
        sr,
        leaves,
        len(tops),
        top_modes.shape[0] // sr,
    )
    got = send_group(send, 1)
    low_keep, low_send = low_call(anc_low, ct, weighted, sr, leaves)
    low_keep, low_send, got = lax.optimization_barrier((low_keep, low_send, got))
    low_got = send_by_core(low_send, (0, 2), (0, 1))
    keep, send = part_call(keep, [got], 2, 1)
    send, weighted = lax.optimization_barrier((send, weighted))
    got = send_by_core(send, (2, 0), (0, 1))
    leaf_proj = proj_call(mt, weighted)
    got, leaf_proj = lax.optimization_barrier((got, leaf_proj))
    keep, *sends = part_call(keep, [got], 4, 1)
    got = [
        send_by_core(x, *there)
        for x, there in zip(sends[::-1], (((0, 3), (2, 2)), ((0, 1), (2, 0)), ((0, 2), (0, 2))))
    ]
    low_keep, got[1] = lax.optimization_barrier((low_keep, got[1]))
    low_keep, low_send = part_call(low_keep, [low_got], 2, 1)
    low_got = send_by_core(low_send, (0, 1), (0, 2))
    total = sum_call(keep, got)
    low_keep, total = lax.optimization_barrier((low_keep, total))
    for bit in range(2, leaves.bit_length() - 1):
        low_keep, low_send = part_call(low_keep, [low_got], 2, 1)
        low_got = send_leaf(low_send, 1 << bit)
        total = sum_call(total, [send_leaf(total, 1 << bit)])
    rels = ((0, 0), (1, 2), (2, 1), (3, 3))
    parts = [total] + [send_by_core(total, (0, even), (0, odd)) for even, odd in rels[1:]]
    new_low = low_end_call(kinv_low, low_keep, low_got)
    new_top = top_end_call(parts, rels, kinv_top, m)
    return (new_top, new_low, leaf_proj)


def solution(mesh):
    both = P(("group", "leaf"), None)
    return jax.shard_map(
        per_device,
        mesh=mesh,
        in_specs=(P("group", None), both, both, both, both, both, both, both, P("group", None), both),
        out_specs=(P("group", None), both, both),
        check_vma=False,
    )
```

```python
import functools

import jax
import jax.numpy as jnp
from jax import lax
from jax.experimental import pallas as pl
from jax.experimental.pallas import tpu as pltpu
from jax.sharding import PartitionSpec as P

BF16, F32 = jnp.bfloat16, jnp.float32
VMEM = pl.BlockSpec(memory_space=pltpu.VMEM)
SMEM = pl.BlockSpec(memory_space=pltpu.SMEM)
HBM = pl.BlockSpec(memory_space=pltpu.HBM)
FILL = 20_000_000_000


def params(mib):
    return pltpu.CompilerParams(vmem_limit_bytes=mib * 2**20)


def cost(flops, moved):
    return pl.CostEstimate(flops=flops, bytes_accessed=moved, transcendentals=0)


def send_group(x, k):
    return lax.ppermute(x, "group", [(i, i ^ k) for i in range(lax.axis_size("group"))])


def send_leaf(x, k):
    return lax.ppermute(x, "leaf", [(i, i ^ k) for i in range(lax.axis_size("leaf"))])


def send_by_core(x, even, odd):
    groups, leaves = lax.axis_size("group"), lax.axis_size("leaf")
    pairs = []
    for g in range(groups):
        far, near = odd if g & 1 else even
        pairs += [(g * leaves + l, (g ^ far) * leaves + (l ^ near)) for l in range(leaves)]
    return lax.ppermute(x, ("group", "leaf"), pairs)


def gather_leaf(x, got):
    rels = [0]
    for bit in range(lax.axis_size("leaf").bit_length() - 2, 1, -1):
        if len(rels) > 1:
            got = send_leaf(x, 1 << bit)
        x = jnp.concatenate([x, got], axis=0)
        rels = rels + [r ^ (1 << bit) for r in rels]
    return [(x, rels, rels)] + [(send_by_core(x, (0, a), (0, b)), [r ^ a for r in rels], [r ^ b for r in rels]) for a, b in ((3, 3), (2, 1), (1, 2))]


def load_kernel(turned, step, *refs):
    n = len(turned)
    sources, copies, turns, sem = refs[:n], refs[n : 2 * n], list(refs[2 * n : -1]), refs[-1]
    pieces = []
    for source, copy, turn in zip(sources, copies, turned):
        out = turns.pop(0) if turn else None
        for i in range(source.shape[0] // step):
            at = slice(i * step, (i + 1) * step)
            move = pltpu.make_async_copy(source.at[at, :], copy.at[at, :], sem.at[len(pieces)])
            move.start()
            pieces.append((move, copy, at, out))
    for move, copy, at, out in pieces:
        move.wait()
        if out is not None:
            out[:, at] = copy[at, :].T


def load_call(arrays, turned):
    shapes = [a.shape for a in arrays] + [a.shape[::-1] for a, t in zip(arrays, turned) if t]
    step = 512
    return pl.pallas_call(
        functools.partial(load_kernel, turned, step),
        in_specs=[HBM] * len(arrays),
        out_specs=[VMEM] * len(shapes),
        out_shape=[pltpu.VMEM(s, BF16) for s in shapes],
        scratch_shapes=[pltpu.SemaphoreType.DMA((sum(a.shape[0] // step for a in arrays),))],
        compiler_params=params(8),
        cost_estimate=cost(FILL, 2 * sum(a.size for a in arrays)),
    )(*[pltpu.with_memory_space_constraint(a, pltpu.HBM) for a in arrays])


def fill_slots(slot_of, anc):
    for b in range(slot_of.shape[0]):
        slot_of[b] = anc.shape[1]
    for j in range(anc.shape[1]):
        slot_of[anc[0, j]] = j


def first_kernel(n_top, anc_top, *refs):
    tops = refs[:n_top]
    coupling, modes, coef, part, slot_top, stacked = refs[n_top:]
    group = lax.axis_index("group")
    slots = anc_top.shape[1]
    sr = stacked.shape[0] // (slots + 1)
    per_group = tops[0].shape[0] // sr
    fill_slots(slot_top, anc_top)
    for r, piece in enumerate(tops):
        for p in range(per_group):
            at = pl.multiple_of(slot_top[(group ^ r) * per_group + p] * sr, sr)
            stacked[pl.ds(at, sr), :] = piece[p * sr : (p + 1) * sr, :]
    step = 512
    for i in range(part.shape[0] // step):
        at = slice(i * step, (i + 1) * step)
        part[at, :] = jnp.dot(modes[at, :], coef[...], preferred_element_type=F32) - jnp.dot(
            coupling[at, : slots * sr], stacked[: slots * sr, :], preferred_element_type=F32
        )


def first_call(anc_top, tops, coupling, modes, coef, sr):
    rows, m = coupling.shape[0], coef.shape[1]
    top_rows = anc_top.shape[1] * sr
    return pl.pallas_call(
        functools.partial(first_kernel, len(tops)),
        in_specs=[SMEM] + [VMEM] * (len(tops) + 3),
        out_specs=VMEM,
        out_shape=jax.ShapeDtypeStruct((rows, m), F32),
        scratch_shapes=[
            pltpu.SMEM((len(tops) * tops[0].shape[0] // sr,), jnp.int32),
            pltpu.VMEM((top_rows + sr, m), BF16),
        ],
        compiler_params=params(8),
        cost_estimate=cost(0, 0),
    )(anc_top, *tops, coupling, modes, coef)


def main_kernel(per_group, low_rels, anc_top, anc_low, *refs):
    n_low = len(low_rels)
    lows = refs[:n_low]
    part, coupling, mass, ct, send, keep, weighted = refs[n_low : n_low + 7]
    slot_top, slot_low, stacked, shapes, loads = refs[n_low + 7 :]
    group, leaf = lax.axis_index("group"), lax.axis_index("leaf")
    top_slots, low_slots = anc_top.shape[1], anc_low.shape[1]
    sr = stacked.shape[0] // (low_slots + 1)
    top_rows = top_slots * sr
    rows = mass.shape[0]
    step = 512

    fill_slots(slot_top, anc_top)
    fill_slots(slot_low, anc_low)
    even = (group & 1) == 0
    for piece, rels in zip(lows, low_rels):
        for p, (r_even, r_odd) in enumerate(zip(*rels)):
            at = pl.multiple_of(slot_low[leaf ^ jnp.where(even, r_even, r_odd)] * sr, sr)
            stacked[pl.ds(at, sr), :] = piece[p * sr : (p + 1) * sr, :]
    for i in range(rows // step):
        at = slice(i * step, (i + 1) * step)
        shapes[at, :] = (
            part[at, :]
            - jnp.dot(coupling[at, top_rows:], stacked[: low_slots * sr, :], preferred_element_type=F32)
        ).astype(BF16)
    for i in range(rows // step):
        at = slice(i * step, (i + 1) * step)
        weighted[at, :] = jnp.dot(mass[at, :], shapes[...], preferred_element_type=F32).astype(BF16)
    width = weighted.shape[1] // 2
    core, near, high = group & 1, leaf & 1, (leaf >> 1) & 1
    for q in range(2):
        loads[q, :top_rows, :] = jnp.dot(
            ct[:top_rows, :], weighted[:, q * width : (q + 1) * width], preferred_element_type=F32
        )
        loads[q, top_rows:, :] = jnp.zeros((sr, width), F32)
    for out, owner in ((keep, core), (send, 1 - core)):
        for first in range(2):
            for second in range(2):
                far = jnp.where(owner == 0, first, second) ^ (group >> 1)
                q = jnp.where(owner == 0, second, first) ^ near
                for p in range(per_group):
                    block = (2 * far + owner) * per_group + (p ^ (high * (per_group // 2)))
                    at = pl.ds(pl.multiple_of(slot_top[block] * sr, sr), sr)
                    to = ((2 * first + second) * per_group + p) * sr
                    out[to : to + sr, :] = loads[q, at, :].astype(out.dtype)


def main_call(anc_top, anc_low, part, lows, low_rels, coupling, mass, ct, sr, leaves, groups, per_group):
    rows, m = part.shape
    half_rows = groups * per_group * sr // 2
    top_rows, low_rows = anc_top.shape[1] * sr, anc_low.shape[1] * sr
    flops = 2 * m * rows * (low_rows + rows + top_rows)
    return pl.pallas_call(
        functools.partial(main_kernel, per_group, low_rels),
        in_specs=[SMEM, SMEM] + [VMEM] * (len(lows) + 4),
        out_specs=[VMEM, VMEM, VMEM],
        out_shape=[
            jax.ShapeDtypeStruct((2 * half_rows, m // 2), BF16),
            jax.ShapeDtypeStruct((2 * half_rows, m // 2), F32),
            jax.ShapeDtypeStruct((rows, m), BF16),
        ],
        scratch_shapes=[
            pltpu.SMEM((groups * per_group,), jnp.int32),
            pltpu.SMEM((leaves,), jnp.int32),
            pltpu.VMEM((low_rows + sr, m), BF16),
            pltpu.VMEM((rows, m), BF16),
            pltpu.VMEM((2, top_rows + sr, m // 2), F32),
        ],
        compiler_params=params(12),
        cost_estimate=cost(flops, 2 * rows * (low_rows + rows)),
    )(anc_top, anc_low, *lows, part, coupling, mass, ct)


def low_kernel(leaves, anc_low, ct, weighted, keep, send, slot_low, loads):
    slots = anc_low.shape[1]
    sr = keep.shape[0] * 2 // leaves
    start = ct.shape[0] - slots * sr
    bits = leaves.bit_length() - 1
    leaf = lax.axis_index("leaf")
    even = (lax.axis_index("group") & 1) == 0
    fill_slots(slot_low, anc_low)
    loads[: slots * sr, :] = jnp.dot(ct[start:, :], weighted[...], preferred_element_type=F32)
    loads[slots * sr :, :] = jnp.zeros((sr, loads.shape[1]), F32)
    for first, out in enumerate((keep, send)):
        for row in range(leaves // 2):
            second = row >> (bits - 2)
            turn = jnp.where(even, 2 * first + second, 2 * second + first)
            for i in range(2, bits):
                turn += ((row >> (bits - 1 - i)) & 1) << i
            at = pl.ds(pl.multiple_of(slot_low[leaf ^ turn] * sr, sr), sr)
            out[row * sr : (row + 1) * sr, :] = loads[at, :].astype(out.dtype)


def proj_kernel(mt, weighted, proj):
    proj[...] = jnp.dot(mt[...], weighted[...], preferred_element_type=F32).astype(BF16)


def proj_call(mt, weighted):
    (modes, rows), m = mt.shape, weighted.shape[1]
    return pl.pallas_call(
        proj_kernel,
        in_specs=[VMEM] * 2,
        out_specs=VMEM,
        out_shape=jax.ShapeDtypeStruct((modes, m), BF16),
        compiler_params=params(4),
        cost_estimate=cost(FILL, 2 * rows * m),
    )(mt, weighted)


def low_call(anc_low, ct, weighted, sr, leaves):
    rows, m = weighted.shape
    kept = leaves // 2 * sr
    low_rows = anc_low.shape[1] * sr
    return pl.pallas_call(
        functools.partial(low_kernel, leaves),
        in_specs=[SMEM, VMEM, VMEM],
        out_specs=[VMEM] * 2,
        out_shape=[jax.ShapeDtypeStruct((kept, m), F32), jax.ShapeDtypeStruct((kept, m), BF16)],
        scratch_shapes=[pltpu.SMEM((leaves,), jnp.int32), pltpu.VMEM((low_rows + sr, m), F32)],
        compiler_params=params(12),
        cost_estimate=cost(2 * m * rows * low_rows, 2 * rows * (low_rows + m)),
    )(anc_low, ct, weighted)


def part_kernel(n_got, keep, *refs):
    got, outs = refs[:n_got], refs[n_got:]
    height, width = outs[0].shape
    n = 0
    for r in range(keep.shape[0] // height):
        for c in range(keep.shape[1] // width):
            at = (slice(r * height, (r + 1) * height), slice(c * width, (c + 1) * width))
            total = keep[at]
            for g in got:
                total += g[at].astype(F32)
            outs[n][...] = total.astype(outs[n].dtype)
            n += 1


def part_call(keep, got, high, wide):
    piece = (keep.shape[0] // high, keep.shape[1] // wide)
    return pl.pallas_call(
        functools.partial(part_kernel, len(got)),
        in_specs=[VMEM] * (1 + len(got)),
        out_specs=[VMEM] * (high * wide),
        out_shape=[jax.ShapeDtypeStruct(piece, F32)] + [jax.ShapeDtypeStruct(piece, BF16)] * (high * wide - 1),
        compiler_params=params(4),
        cost_estimate=cost(keep.size, 8 * keep.size),
    )(keep, *got)


def quarter_kernel(keep, got, own, near, other, across):
    even = (lax.axis_index("group") & 1) == 0
    n = own.shape[0]
    for out, at in (
        (own, 0),
        (near, jnp.where(even, 2 * n, n)),
        (other, jnp.where(even, n, 2 * n)),
        (across, 3 * n),
    ):
        at = pl.ds(pl.multiple_of(at, n), n)
        out[...] = (keep[at, :] + got[at, :].astype(F32)).astype(out.dtype)


def quarter_call(keep, got):
    piece = (keep.shape[0] // 4, keep.shape[1])
    return pl.pallas_call(
        quarter_kernel,
        in_specs=[VMEM] * 2,
        out_specs=[VMEM] * 4,
        out_shape=[jax.ShapeDtypeStruct(piece, F32)] + [jax.ShapeDtypeStruct(piece, BF16)] * 3,
        compiler_params=params(4),
        cost_estimate=cost(keep.size, 8 * keep.size),
    )(keep, got)


def sum_kernel(keep, *refs):
    total = keep[...].astype(F32)
    for got in refs[:-1]:
        total += got[...].astype(F32)
    refs[-1][...] = total.astype(BF16)


def sum_call(keep, got):
    return pl.pallas_call(
        sum_kernel,
        in_specs=[VMEM] * (1 + len(got)),
        out_specs=VMEM,
        out_shape=jax.ShapeDtypeStruct(keep.shape, BF16),
        compiler_params=params(4),
        cost_estimate=cost(keep.size, 8 * keep.size),
    )(keep, *got)


def solve(kinv, loads):
    def parts(x):
        coarse = x.astype(BF16)
        fine = (x - coarse.astype(F32)).astype(BF16)
        return coarse, fine, (x - coarse.astype(F32) - fine.astype(F32)).astype(BF16)

    n = kinv.shape[0]
    total = None
    for i, part in enumerate(parts(loads) if loads.dtype == F32 else (loads,)):
        left = jnp.concatenate(parts(kinv)[: 3 - i], axis=0)
        product = jnp.dot(left, part, preferred_element_type=F32)
        for k in range(3 - i):
            term = product[k * n : (k + 1) * n]
            total = term if total is None else total + term
    return total


def low_end_kernel(kinv, keep, got, out):
    out[...] = solve(kinv[...], keep[...] + got[...].astype(F32))


def low_end_call(kinv, keep, got):
    return pl.pallas_call(
        low_end_kernel,
        in_specs=[VMEM] * 3,
        out_specs=VMEM,
        out_shape=jax.ShapeDtypeStruct(keep.shape, F32),
        compiler_params=params(4),
        cost_estimate=cost(12 * keep.size * 64, 8 * keep.size),
    )(kinv, keep, got)


def top_end_kernel(rels, kinv, *refs):
    parts, out, loads = refs[:-2], refs[-2], refs[-1]
    leaf = lax.axis_index("leaf")
    even = (lax.axis_index("group") & 1) == 0
    sr = kinv.shape[1]
    for part, (r_even, r_odd) in zip(parts, rels):
        height, width = part.shape
        there = leaf ^ jnp.where(even, r_even, r_odd)
        row = pl.multiple_of(((there >> 1) & 1) * height, height)
        col = pl.multiple_of((there & 1) * width, 128)
        loads[pl.ds(row, height), pl.ds(col, width)] = part[...]
    for b in range(out.shape[0] // sr):
        at = slice(b * sr, (b + 1) * sr)
        out[at, :] = solve(kinv[at, :], loads[at, :])


def top_end_call(parts, rels, kinv, m):
    rows = kinv.shape[0]
    return pl.pallas_call(
        functools.partial(top_end_kernel, rels),
        in_specs=[VMEM] * (1 + len(parts)),
        out_specs=VMEM,
        out_shape=jax.ShapeDtypeStruct((rows, m), F32),
        scratch_shapes=[pltpu.VMEM((rows, m), BF16)],
        compiler_params=params(8),
        cost_estimate=cost(12 * rows * m * 64, 8 * rows * m),
    )(kinv, *parts)


def per_device(
    top_modes, low_modes, anc_top, anc_low, coupling, leaf_mass, leaf_modes, leaf_coef, kinv_top, kinv_low
):
    sr = kinv_low.shape[1]
    m = low_modes.shape[1]
    leaves = lax.axis_size("leaf")
    near_top = send_group(top_modes, 1)
    far_low = send_leaf(low_modes, leaves // 2)
    near_top, to_send = lax.optimization_barrier((near_top, top_modes))
    far_top = send_group(to_send, 2)
    leaf_modes, mt = load_call((leaf_modes,), (True,))
    far_low, mt = lax.optimization_barrier((far_low, mt))
    held = gather_leaf(low_modes, far_low)
    coupling, ct = load_call((coupling,), (True,))
    tops = [top_modes, near_top, far_top, send_group(far_top, 1)]
    part = first_call(anc_top, tops, coupling, leaf_modes, leaf_coef, sr)
    send, keep, weighted = main_call(
        anc_top,
        anc_low,
        part,
        [h[0] for h in held],
        [h[1:] for h in held],
        coupling,
        leaf_mass,
        ct,
        sr,
        leaves,
        len(tops),
        top_modes.shape[0] // sr,
    )
    got = send_group(send, 1)
    low_keep, low_send = low_call(anc_low, ct, weighted, sr, leaves)
    low_keep, low_send, got = lax.optimization_barrier((low_keep, low_send, got))
    low_got = send_by_core(low_send, (0, 2), (0, 1))
    keep, send = part_call(keep, [got], 2, 1)
    send, weighted = lax.optimization_barrier((send, weighted))
    got = send_by_core(send, (2, 0), (0, 1))
    leaf_proj = proj_call(mt, weighted)
    got, leaf_proj = lax.optimization_barrier((got, leaf_proj))
    keep, near, other, across = quarter_call(keep, got)
    got = [send_by_core(x, *there) for x, *there in ((across, (0, 3), (2, 2)), (other, (0, 2), (2, 0)), (near, (0, 1), (0, 2)))]
    low_keep, got[1] = lax.optimization_barrier((low_keep, got[1]))
    low_keep, low_send = part_call(low_keep, [low_got], 2, 1)
    low_got = send_by_core(low_send, (0, 1), (0, 2))
    total = sum_call(keep, got)
    low_keep, total = lax.optimization_barrier((low_keep, total))
    for bit in range(2, leaves.bit_length() - 1):
        low_keep, low_send = part_call(low_keep, [low_got], 2, 1)
        low_got = send_leaf(low_send, 1 << bit)
        total = sum_call(total, [send_leaf(total, 1 << bit)])
    rels = ((0, 0), (1, 2), (2, 1), (3, 3))
    parts = [total] + [send_by_core(total, (0, even), (0, odd)) for even, odd in rels[1:]]
    new_low = low_end_call(kinv_low, low_keep, low_got)
    new_top = top_end_call(parts, rels, kinv_top, m)
    return (new_top, new_low, leaf_proj)


def solution(mesh):
    both = P(("group", "leaf"), None)
    return jax.shard_map(
        per_device,
        mesh=mesh,
        in_specs=(P("group", None), both, both, both, both, both, both, both, P("group", None), both),
        out_specs=(P("group", None), both, both),
        check_vma=False,
    )
```

```python
import functools

import jax
import jax.numpy as jnp
from jax import lax
from jax.experimental import pallas as pl
from jax.experimental.pallas import tpu as pltpu
from jax.sharding import PartitionSpec as P

BF16, F32 = jnp.bfloat16, jnp.float32
VMEM = pl.BlockSpec(memory_space=pltpu.VMEM)
SMEM = pl.BlockSpec(memory_space=pltpu.SMEM)
HBM = pl.BlockSpec(memory_space=pltpu.HBM)
FILL = 20_000_000_000


def params(mib):
    return pltpu.CompilerParams(vmem_limit_bytes=mib * 2**20)


def cost(flops, moved):
    return pl.CostEstimate(flops=flops, bytes_accessed=moved, transcendentals=0)


def send_group(x, k):
    return lax.ppermute(x, "group", [(i, i ^ k) for i in range(lax.axis_size("group"))])


def send_leaf(x, k):
    return lax.ppermute(x, "leaf", [(i, i ^ k) for i in range(lax.axis_size("leaf"))])


def send_by_core(x, even, odd):
    groups, leaves = lax.axis_size("group"), lax.axis_size("leaf")
    pairs = []
    for g in range(groups):
        far, near = odd if g & 1 else even
        pairs += [(g * leaves + l, (g ^ far) * leaves + (l ^ near)) for l in range(leaves)]
    return lax.ppermute(x, ("group", "leaf"), pairs)


def gather_leaf(x, got):
    rels = [0]
    for bit in range(lax.axis_size("leaf").bit_length() - 2, 1, -1):
        if len(rels) > 1:
            got = send_leaf(x, 1 << bit)
        x = jnp.concatenate([x, got], axis=0)
        rels = rels + [r ^ (1 << bit) for r in rels]
    return [(x, rels, rels)] + [(send_by_core(x, (0, a), (0, b)), [r ^ a for r in rels], [r ^ b for r in rels]) for a, b in ((3, 3), (2, 1), (1, 2))]


def load_kernel(turned, step, *refs):
    n = len(turned)
    sources, copies, turns, sem = refs[:n], refs[n : 2 * n], list(refs[2 * n : -1]), refs[-1]
    pieces = []
    for source, copy, turn in zip(sources, copies, turned):
        out = turns.pop(0) if turn else None
        for i in range(source.shape[0] // step):
            at = slice(i * step, (i + 1) * step)
            move = pltpu.make_async_copy(source.at[at, :], copy.at[at, :], sem.at[len(pieces)])
            move.start()
            pieces.append((move, copy, at, out))
    for move, copy, at, out in pieces:
        move.wait()
        if out is not None:
            out[:, at] = copy[at, :].T


def load_call(arrays, turned):
    shapes = [a.shape for a in arrays] + [a.shape[::-1] for a, t in zip(arrays, turned) if t]
    step = 512
    return pl.pallas_call(
        functools.partial(load_kernel, turned, step),
        in_specs=[HBM] * len(arrays),
        out_specs=[VMEM] * len(shapes),
        out_shape=[pltpu.VMEM(s, BF16) for s in shapes],
        scratch_shapes=[pltpu.SemaphoreType.DMA((sum(a.shape[0] // step for a in arrays),))],
        compiler_params=params(8),
        cost_estimate=cost(FILL, 2 * sum(a.size for a in arrays)),
    )(*[pltpu.with_memory_space_constraint(a, pltpu.HBM) for a in arrays])


def fill_slots(slot_of, anc):
    for b in range(slot_of.shape[0]):
        slot_of[b] = anc.shape[1]
    for j in range(anc.shape[1]):
        slot_of[anc[0, j]] = j


def first_kernel(n_top, anc_top, *refs):
    tops = refs[:n_top]
    coupling, modes, coef, part, slot_top, stacked = refs[n_top:]
    group = lax.axis_index("group")
    slots = anc_top.shape[1]
    sr = stacked.shape[0] // (slots + 1)
    per_group = tops[0].shape[0] // sr
    fill_slots(slot_top, anc_top)
    for r, piece in enumerate(tops):
        for p in range(per_group):
            at = pl.multiple_of(slot_top[(group ^ r) * per_group + p] * sr, sr)
            stacked[pl.ds(at, sr), :] = piece[p * sr : (p + 1) * sr, :]
    step = 512
    for i in range(part.shape[0] // step):
        at = slice(i * step, (i + 1) * step)
        part[at, :] = jnp.dot(modes[at, :], coef[...], preferred_element_type=F32) - jnp.dot(
            coupling[at, : slots * sr], stacked[: slots * sr, :], preferred_element_type=F32
        )


def first_call(anc_top, tops, coupling, modes, coef, sr):
    rows, m = coupling.shape[0], coef.shape[1]
    top_rows = anc_top.shape[1] * sr
    return pl.pallas_call(
        functools.partial(first_kernel, len(tops)),
        in_specs=[SMEM] + [VMEM] * (len(tops) + 3),
        out_specs=VMEM,
        out_shape=jax.ShapeDtypeStruct((rows, m), F32),
        scratch_shapes=[
            pltpu.SMEM((len(tops) * tops[0].shape[0] // sr,), jnp.int32),
            pltpu.VMEM((top_rows + sr, m), BF16),
        ],
        compiler_params=params(8),
        cost_estimate=cost(0, 0),
    )(anc_top, *tops, coupling, modes, coef)


def main_kernel(per_group, low_rels, anc_top, anc_low, *refs):
    n_low = len(low_rels)
    lows = refs[:n_low]
    part, coupling, mass, ct, send, keep, weighted = refs[n_low : n_low + 7]
    slot_top, slot_low, stacked, shapes, loads = refs[n_low + 7 :]
    group, leaf = lax.axis_index("group"), lax.axis_index("leaf")
    top_slots, low_slots = anc_top.shape[1], anc_low.shape[1]
    sr = stacked.shape[0] // (low_slots + 1)
    top_rows = top_slots * sr
    rows = mass.shape[0]
    step = 512

    fill_slots(slot_top, anc_top)
    fill_slots(slot_low, anc_low)
    even = (group & 1) == 0
    for piece, rels in zip(lows, low_rels):
        for p, (r_even, r_odd) in enumerate(zip(*rels)):
            at = pl.multiple_of(slot_low[leaf ^ jnp.where(even, r_even, r_odd)] * sr, sr)
            stacked[pl.ds(at, sr), :] = piece[p * sr : (p + 1) * sr, :]
    for i in range(rows // step):
        at = slice(i * step, (i + 1) * step)
        shapes[at, :] = (
            part[at, :]
            - jnp.dot(coupling[at, top_rows:], stacked[: low_slots * sr, :], preferred_element_type=F32)
        ).astype(BF16)
    for i in range(rows // step):
        at = slice(i * step, (i + 1) * step)
        weighted[at, :] = jnp.dot(mass[at, :], shapes[...], preferred_element_type=F32).astype(BF16)
    width = weighted.shape[1] // 2
    core, near, high = group & 1, leaf & 1, (leaf >> 1) & 1
    for q in range(2):
        loads[q, :top_rows, :] = jnp.dot(
            ct[:top_rows, :], weighted[:, q * width : (q + 1) * width], preferred_element_type=F32
        )
        loads[q, top_rows:, :] = jnp.zeros((sr, width), F32)
    for out, owner in ((keep, core), (send, 1 - core)):
        for first in range(2):
            for second in range(2):
                far = jnp.where(owner == 0, first, second) ^ (group >> 1)
                q = jnp.where(owner == 0, second, first) ^ near
                for p in range(per_group):
                    block = (2 * far + owner) * per_group + (p ^ (high * (per_group // 2)))
                    at = pl.ds(pl.multiple_of(slot_top[block] * sr, sr), sr)
                    to = ((2 * first + second) * per_group + p) * sr
                    out[to : to + sr, :] = loads[q, at, :].astype(out.dtype)


def main_call(anc_top, anc_low, part, lows, low_rels, coupling, mass, ct, sr, leaves, groups, per_group):
    rows, m = part.shape
    half_rows = groups * per_group * sr // 2
    top_rows, low_rows = anc_top.shape[1] * sr, anc_low.shape[1] * sr
    flops = 2 * m * rows * (low_rows + rows + top_rows)
    return pl.pallas_call(
        functools.partial(main_kernel, per_group, low_rels),
        in_specs=[SMEM, SMEM] + [VMEM] * (len(lows) + 4),
        out_specs=[VMEM, VMEM, VMEM],
        out_shape=[
            jax.ShapeDtypeStruct((2 * half_rows, m // 2), BF16),
            jax.ShapeDtypeStruct((2 * half_rows, m // 2), F32),
            jax.ShapeDtypeStruct((rows, m), BF16),
        ],
        scratch_shapes=[
            pltpu.SMEM((groups * per_group,), jnp.int32),
            pltpu.SMEM((leaves,), jnp.int32),
            pltpu.VMEM((low_rows + sr, m), BF16),
            pltpu.VMEM((rows, m), BF16),
            pltpu.VMEM((2, top_rows + sr, m // 2), F32),
        ],
        compiler_params=params(12),
        cost_estimate=cost(flops, 2 * rows * (low_rows + rows)),
    )(anc_top, anc_low, *lows, part, coupling, mass, ct)


def low_kernel(leaves, anc_low, ct, weighted, keep, send, slot_low, loads):
    slots = anc_low.shape[1]
    sr = keep.shape[0] * 2 // leaves
    start = ct.shape[0] - slots * sr
    bits = leaves.bit_length() - 1
    leaf = lax.axis_index("leaf")
    even = (lax.axis_index("group") & 1) == 0
    fill_slots(slot_low, anc_low)
    loads[: slots * sr, :] = jnp.dot(ct[start:, :], weighted[...], preferred_element_type=F32)
    loads[slots * sr :, :] = jnp.zeros((sr, loads.shape[1]), F32)
    for first, out in enumerate((keep, send)):
        for row in range(leaves // 2):
            second = row >> (bits - 2)
            turn = jnp.where(even, 2 * first + second, 2 * second + first)
            for i in range(2, bits):
                turn += ((row >> (bits - 1 - i)) & 1) << i
            at = pl.ds(pl.multiple_of(slot_low[leaf ^ turn] * sr, sr), sr)
            out[row * sr : (row + 1) * sr, :] = loads[at, :].astype(out.dtype)


def proj_kernel(mt, weighted, proj):
    proj[...] = jnp.dot(mt[...], weighted[...], preferred_element_type=F32).astype(BF16)


def proj_call(mt, weighted):
    (modes, rows), m = mt.shape, weighted.shape[1]
    return pl.pallas_call(
        proj_kernel,
        in_specs=[VMEM] * 2,
        out_specs=VMEM,
        out_shape=jax.ShapeDtypeStruct((modes, m), BF16),
        compiler_params=params(4),
        cost_estimate=cost(FILL, 2 * rows * m),
    )(mt, weighted)


def low_call(anc_low, ct, weighted, sr, leaves):
    rows, m = weighted.shape
    kept = leaves // 2 * sr
    low_rows = anc_low.shape[1] * sr
    return pl.pallas_call(
        functools.partial(low_kernel, leaves),
        in_specs=[SMEM, VMEM, VMEM],
        out_specs=[VMEM] * 2,
        out_shape=[jax.ShapeDtypeStruct((kept, m), F32), jax.ShapeDtypeStruct((kept, m), BF16)],
        scratch_shapes=[pltpu.SMEM((leaves,), jnp.int32), pltpu.VMEM((low_rows + sr, m), F32)],
        compiler_params=params(12),
        cost_estimate=cost(2 * m * rows * low_rows, 2 * rows * (low_rows + m)),
    )(anc_low, ct, weighted)


def part_kernel(n_got, keep, *refs):
    got, outs = refs[:n_got], refs[n_got:]
    height, width = outs[0].shape
    n = 0
    for r in range(keep.shape[0] // height):
        for c in range(keep.shape[1] // width):
            at = (slice(r * height, (r + 1) * height), slice(c * width, (c + 1) * width))
            total = keep[at]
            for g in got:
                total += g[at].astype(F32)
            outs[n][...] = total.astype(outs[n].dtype)
            n += 1


def part_call(keep, got, high, wide):
    piece = (keep.shape[0] // high, keep.shape[1] // wide)
    return pl.pallas_call(
        functools.partial(part_kernel, len(got)),
        in_specs=[VMEM] * (1 + len(got)),
        out_specs=[VMEM] * (high * wide),
        out_shape=[jax.ShapeDtypeStruct(piece, F32)] + [jax.ShapeDtypeStruct(piece, BF16)] * (high * wide - 1),
        compiler_params=params(4),
        cost_estimate=cost(keep.size, 8 * keep.size),
    )(keep, *got)


def quarter_kernel(keep, got, own, near, other, across):
    even = (lax.axis_index("group") & 1) == 0
    n = own.shape[0]
    for out, at in (
        (own, 0),
        (near, jnp.where(even, 2 * n, n)),
        (other, jnp.where(even, n, 2 * n)),
        (across, 3 * n),
    ):
        at = pl.ds(pl.multiple_of(at, n), n)
        out[...] = (keep[at, :] + got[at, :].astype(F32)).astype(out.dtype)


def quarter_call(keep, got):
    piece = (keep.shape[0] // 4, keep.shape[1])
    return pl.pallas_call(
        quarter_kernel,
        in_specs=[VMEM] * 2,
        out_specs=[VMEM] * 4,
        out_shape=[jax.ShapeDtypeStruct(piece, F32)] + [jax.ShapeDtypeStruct(piece, BF16)] * 3,
        compiler_params=params(4),
        cost_estimate=cost(keep.size, 8 * keep.size),
    )(keep, got)


def sum_kernel(keep, *refs):
    total = keep[...].astype(F32)
    for got in refs[:-1]:
        total += got[...].astype(F32)
    refs[-1][...] = total.astype(BF16)


def sum_call(keep, got):
    return pl.pallas_call(
        sum_kernel,
        in_specs=[VMEM] * (1 + len(got)),
        out_specs=VMEM,
        out_shape=jax.ShapeDtypeStruct(keep.shape, BF16),
        compiler_params=params(4),
        cost_estimate=cost(keep.size, 8 * keep.size),
    )(keep, *got)


def solve(kinv, loads):
    def parts(x):
        coarse = x.astype(BF16)
        fine = (x - coarse.astype(F32)).astype(BF16)
        return coarse, fine, (x - coarse.astype(F32) - fine.astype(F32)).astype(BF16)

    n = kinv.shape[0]
    total = None
    for i, part in enumerate(parts(loads) if loads.dtype == F32 else (loads,)):
        left = jnp.concatenate(parts(kinv)[: 3 - i], axis=0)
        product = jnp.dot(left, part, preferred_element_type=F32)
        for k in range(3 - i):
            term = product[k * n : (k + 1) * n]
            total = term if total is None else total + term
    return total


def low_end_kernel(kinv, keep, got, out):
    out[...] = solve(kinv[...], keep[...] + got[...].astype(F32))


def low_end_call(kinv, keep, got):
    return pl.pallas_call(
        low_end_kernel,
        in_specs=[VMEM] * 3,
        out_specs=VMEM,
        out_shape=jax.ShapeDtypeStruct(keep.shape, F32),
        compiler_params=params(4),
        cost_estimate=cost(12 * keep.size * 64, 8 * keep.size),
    )(kinv, keep, got)


def solve_kernel(kinv, keep, got, out):
    sr, height = kinv.shape[1], out.shape[0]
    high = (lax.axis_index("leaf") >> 1) & 1
    loads = (keep[...].astype(F32) + got[...].astype(F32)).astype(BF16)
    for b in range(height // sr):
        at = pl.ds(pl.multiple_of(high * height + b * sr, sr), sr)
        out[b * sr : (b + 1) * sr, :] = solve(kinv[at, :], loads[b * sr : (b + 1) * sr]).astype(BF16)


def solve_call(kinv, keep, got):
    return pl.pallas_call(
        solve_kernel,
        in_specs=[VMEM] * 3,
        out_specs=VMEM,
        out_shape=jax.ShapeDtypeStruct(keep.shape, BF16),
        compiler_params=params(4),
        cost_estimate=cost(12 * keep.size * 64, 8 * keep.size),
    )(kinv, keep, got)


def top_end_kernel(rels, *refs):
    parts, out = refs[:-1], refs[-1]
    leaf = lax.axis_index("leaf")
    even = (lax.axis_index("group") & 1) == 0
    for part, (r_even, r_odd) in zip(parts, rels):
        height, width = part.shape
        there = leaf ^ jnp.where(even, r_even, r_odd)
        row = pl.multiple_of(((there >> 1) & 1) * height, height)
        col = pl.multiple_of((there & 1) * width, 128)
        out[pl.ds(row, height), pl.ds(col, width)] = part[...].astype(F32)


def top_end_call(parts, rels, rows, m):
    return pl.pallas_call(
        functools.partial(top_end_kernel, rels),
        in_specs=[VMEM] * len(parts),
        out_specs=VMEM,
        out_shape=jax.ShapeDtypeStruct((rows, m), F32),
        compiler_params=params(8),
        cost_estimate=cost(rows * m, 6 * rows * m),
    )(*parts)


def per_device(
    top_modes, low_modes, anc_top, anc_low, coupling, leaf_mass, leaf_modes, leaf_coef, kinv_top, kinv_low
):
    sr = kinv_low.shape[1]
    m = low_modes.shape[1]
    leaves = lax.axis_size("leaf")
    near_top = send_group(top_modes, 1)
    far_low = send_leaf(low_modes, leaves // 2)
    near_top, to_send = lax.optimization_barrier((near_top, top_modes))
    far_top = send_group(to_send, 2)
    leaf_modes, mt = load_call((leaf_modes,), (True,))
    far_low, mt = lax.optimization_barrier((far_low, mt))
    held = gather_leaf(low_modes, far_low)
    coupling, ct = load_call((coupling,), (True,))
    tops = [top_modes, near_top, far_top, send_group(far_top, 1)]
    part = first_call(anc_top, tops, coupling, leaf_modes, leaf_coef, sr)
    send, keep, weighted = main_call(
        anc_top,
        anc_low,
        part,
        [h[0] for h in held],
        [h[1:] for h in held],
        coupling,
        leaf_mass,
        ct,
        sr,
        leaves,
        len(tops),
        top_modes.shape[0] // sr,
    )
    got = send_group(send, 1)
    low_keep, low_send = low_call(anc_low, ct, weighted, sr, leaves)
    low_keep, low_send, got = lax.optimization_barrier((low_keep, low_send, got))
    low_got = send_by_core(low_send, (0, 2), (0, 1))
    keep, send = part_call(keep, [got], 2, 1)
    send, weighted = lax.optimization_barrier((send, weighted))
    got = send_by_core(send, (2, 0), (0, 1))
    leaf_proj = proj_call(mt, weighted)
    got, leaf_proj = lax.optimization_barrier((got, leaf_proj))
    keep, near, other, across = quarter_call(keep, got)
    got = [send_by_core(x, *there) for x, *there in ((other, (0, 2), (2, 0)), (across, (0, 3), (2, 2)), (near, (0, 1), (0, 2)))]
    low_keep, got[0] = lax.optimization_barrier((low_keep, got[0]))
    low_keep, low_send = part_call(low_keep, [low_got], 2, 1)
    low_got = send_by_core(low_send, (0, 1), (0, 2))
    total = sum_call(keep, got)
    low_keep, total = lax.optimization_barrier((low_keep, total))
    for bit in range(2, leaves.bit_length() - 1):
        low_keep, low_send = part_call(low_keep, [low_got], 2, 1)
        low_got = send_leaf(low_send, 1 << bit)
        got = send_leaf(total, 1 << bit)
        if bit == leaves.bit_length() - 2:
            total = solve_call(kinv_top, total, got)
        else:
            total = sum_call(total, [got])
    rels = ((0, 0), (3, 3), (2, 1), (1, 2))
    parts = [total] + [send_by_core(total, (0, even), (0, odd)) for even, odd in rels[1:]]
    new_low = low_end_call(kinv_low, low_keep, low_got)
    new_top = top_end_call(parts, rels, kinv_top.shape[0], m)
    return (new_top, new_low, leaf_proj)


def solution(mesh):
    both = P(("group", "leaf"), None)
    return jax.shard_map(
        per_device,
        mesh=mesh,
        in_specs=(P("group", None), both, both, both, both, both, both, both, P("group", None), both),
        out_specs=(P("group", None), both, both),
        check_vma=False,
    )
```

```python
import functools

import jax
import jax.numpy as jnp
from jax import lax
from jax.experimental import pallas as pl
from jax.experimental.pallas import tpu as pltpu
from jax.sharding import PartitionSpec as P

BF16, F32 = jnp.bfloat16, jnp.float32
VMEM = pl.BlockSpec(memory_space=pltpu.VMEM)
SMEM = pl.BlockSpec(memory_space=pltpu.SMEM)
HBM = pl.BlockSpec(memory_space=pltpu.HBM)
FILL = 20_000_000_000


def params(mib):
    return pltpu.CompilerParams(vmem_limit_bytes=mib * 2**20)


def cost(flops, moved):
    return pl.CostEstimate(flops=flops, bytes_accessed=moved, transcendentals=0)


def send_group(x, k):
    return lax.ppermute(x, "group", [(i, i ^ k) for i in range(lax.axis_size("group"))])


def send_leaf(x, k):
    return lax.ppermute(x, "leaf", [(i, i ^ k) for i in range(lax.axis_size("leaf"))])


def send_by_core(x, even, odd):
    groups, leaves = lax.axis_size("group"), lax.axis_size("leaf")
    pairs = []
    for g in range(groups):
        far, near = odd if g & 1 else even
        pairs += [(g * leaves + l, (g ^ far) * leaves + (l ^ near)) for l in range(leaves)]
    return lax.ppermute(x, ("group", "leaf"), pairs)


def gather_leaf(x, got):
    rels = [0]
    for bit in range(lax.axis_size("leaf").bit_length() - 2, 1, -1):
        if len(rels) > 1:
            got = send_leaf(x, 1 << bit)
        x = jnp.concatenate([x, got], axis=0)
        rels = rels + [r ^ (1 << bit) for r in rels]
    return [(x, rels, rels)] + [(send_by_core(x, (0, a), (0, b)), [r ^ a for r in rels], [r ^ b for r in rels]) for a, b in ((3, 3), (2, 1), (1, 2))]


def load_kernel(turned, step, *refs):
    n = len(turned)
    sources, copies, turns, sem = refs[:n], refs[n : 2 * n], list(refs[2 * n : -1]), refs[-1]
    pieces = []
    for source, copy, turn in zip(sources, copies, turned):
        out = turns.pop(0) if turn else None
        for i in range(source.shape[0] // step):
            at = slice(i * step, (i + 1) * step)
            move = pltpu.make_async_copy(source.at[at, :], copy.at[at, :], sem.at[len(pieces)])
            move.start()
            pieces.append((move, copy, at, out))
    for move, copy, at, out in pieces:
        move.wait()
        if out is not None:
            out[:, at] = copy[at, :].T


def load_call(arrays, turned):
    shapes = [a.shape for a in arrays] + [a.shape[::-1] for a, t in zip(arrays, turned) if t]
    step = 512
    return pl.pallas_call(
        functools.partial(load_kernel, turned, step),
        in_specs=[HBM] * len(arrays),
        out_specs=[VMEM] * len(shapes),
        out_shape=[pltpu.VMEM(s, BF16) for s in shapes],
        scratch_shapes=[pltpu.SemaphoreType.DMA((sum(a.shape[0] // step for a in arrays),))],
        compiler_params=params(8),
        cost_estimate=cost(FILL, 2 * sum(a.size for a in arrays)),
    )(*[pltpu.with_memory_space_constraint(a, pltpu.HBM) for a in arrays])


def fill_slots(slot_of, anc):
    for b in range(slot_of.shape[0]):
        slot_of[b] = anc.shape[1]
    for j in range(anc.shape[1]):
        slot_of[anc[0, j]] = j


def first_kernel(n_top, anc_top, *refs):
    tops = refs[:n_top]
    coupling, modes, coef, part, slot_top, stacked = refs[n_top:]
    group = lax.axis_index("group")
    slots = anc_top.shape[1]
    sr = stacked.shape[0] // (slots + 1)
    per_group = tops[0].shape[0] // sr
    fill_slots(slot_top, anc_top)
    for r, piece in enumerate(tops):
        for p in range(per_group):
            at = pl.multiple_of(slot_top[(group ^ r) * per_group + p] * sr, sr)
            stacked[pl.ds(at, sr), :] = piece[p * sr : (p + 1) * sr, :]
    step = 512
    for i in range(part.shape[0] // step):
        at = slice(i * step, (i + 1) * step)
        part[at, :] = jnp.dot(modes[at, :], coef[...], preferred_element_type=F32) - jnp.dot(
            coupling[at, : slots * sr], stacked[: slots * sr, :], preferred_element_type=F32
        )


def first_call(anc_top, tops, coupling, modes, coef, sr):
    rows, m = coupling.shape[0], coef.shape[1]
    top_rows = anc_top.shape[1] * sr
    return pl.pallas_call(
        functools.partial(first_kernel, len(tops)),
        in_specs=[SMEM] + [VMEM] * (len(tops) + 3),
        out_specs=VMEM,
        out_shape=jax.ShapeDtypeStruct((rows, m), F32),
        scratch_shapes=[
            pltpu.SMEM((len(tops) * tops[0].shape[0] // sr,), jnp.int32),
            pltpu.VMEM((top_rows + sr, m), BF16),
        ],
        compiler_params=params(8),
        cost_estimate=cost(0, 0),
    )(anc_top, *tops, coupling, modes, coef)


def main_kernel(per_group, low_rels, anc_top, anc_low, *refs):
    n_low = len(low_rels)
    lows = refs[:n_low]
    part, coupling, mass, ct, send, keep, weighted = refs[n_low : n_low + 7]
    slot_top, slot_low, stacked, shapes, loads = refs[n_low + 7 :]
    group, leaf = lax.axis_index("group"), lax.axis_index("leaf")
    top_slots, low_slots = anc_top.shape[1], anc_low.shape[1]
    sr = stacked.shape[0] // (low_slots + 1)
    top_rows = top_slots * sr
    rows = mass.shape[0]
    step = 512

    fill_slots(slot_top, anc_top)
    fill_slots(slot_low, anc_low)
    even = (group & 1) == 0
    for piece, rels in zip(lows, low_rels):
        for p, (r_even, r_odd) in enumerate(zip(*rels)):
            at = pl.multiple_of(slot_low[leaf ^ jnp.where(even, r_even, r_odd)] * sr, sr)
            stacked[pl.ds(at, sr), :] = piece[p * sr : (p + 1) * sr, :]
    for i in range(rows // step):
        at = slice(i * step, (i + 1) * step)
        shapes[at, :] = (
            part[at, :]
            - jnp.dot(coupling[at, top_rows:], stacked[: low_slots * sr, :], preferred_element_type=F32)
        ).astype(BF16)
    for i in range(rows // step):
        at = slice(i * step, (i + 1) * step)
        weighted[at, :] = jnp.dot(mass[at, :], shapes[...], preferred_element_type=F32).astype(BF16)
    width = weighted.shape[1] // 2
    core, near, high = group & 1, leaf & 1, (leaf >> 1) & 1
    for q in range(2):
        loads[q, :top_rows, :] = jnp.dot(
            ct[:top_rows, :], weighted[:, q * width : (q + 1) * width], preferred_element_type=F32
        )
        loads[q, top_rows:, :] = jnp.zeros((sr, width), F32)
    for out, owner in ((keep, core), (send, 1 - core)):
        for first in range(2):
            for second in range(2):
                far = jnp.where(owner == 0, first, second) ^ (group >> 1)
                q = jnp.where(owner == 0, second, first) ^ near
                for p in range(per_group):
                    block = (2 * far + owner) * per_group + (p ^ (high * (per_group // 2)))
                    at = pl.ds(pl.multiple_of(slot_top[block] * sr, sr), sr)
                    to = ((2 * first + second) * per_group + p) * sr
                    out[to : to + sr, :] = loads[q, at, :].astype(out.dtype)


def main_call(anc_top, anc_low, part, lows, low_rels, coupling, mass, ct, sr, leaves, groups, per_group):
    rows, m = part.shape
    half_rows = groups * per_group * sr // 2
    top_rows, low_rows = anc_top.shape[1] * sr, anc_low.shape[1] * sr
    flops = 2 * m * rows * (low_rows + rows + top_rows)
    return pl.pallas_call(
        functools.partial(main_kernel, per_group, low_rels),
        in_specs=[SMEM, SMEM] + [VMEM] * (len(lows) + 4),
        out_specs=[VMEM, VMEM, VMEM],
        out_shape=[
            jax.ShapeDtypeStruct((2 * half_rows, m // 2), BF16),
            jax.ShapeDtypeStruct((2 * half_rows, m // 2), F32),
            jax.ShapeDtypeStruct((rows, m), BF16),
        ],
        scratch_shapes=[
            pltpu.SMEM((groups * per_group,), jnp.int32),
            pltpu.SMEM((leaves,), jnp.int32),
            pltpu.VMEM((low_rows + sr, m), BF16),
            pltpu.VMEM((rows, m), BF16),
            pltpu.VMEM((2, top_rows + sr, m // 2), F32),
        ],
        compiler_params=params(12),
        cost_estimate=cost(flops, 2 * rows * (low_rows + rows)),
    )(anc_top, anc_low, *lows, part, coupling, mass, ct)


def low_kernel(leaves, anc_low, ct, weighted, keep, send, slot_low, loads):
    slots = anc_low.shape[1]
    sr = keep.shape[0] * 2 // leaves
    start = ct.shape[0] - slots * sr
    bits = leaves.bit_length() - 1
    leaf = lax.axis_index("leaf")
    even = (lax.axis_index("group") & 1) == 0
    fill_slots(slot_low, anc_low)
    loads[: slots * sr, :] = jnp.dot(ct[start:, :], weighted[...], preferred_element_type=F32)
    loads[slots * sr :, :] = jnp.zeros((sr, loads.shape[1]), F32)
    for first, out in enumerate((keep, send)):
        for row in range(leaves // 2):
            second = row >> (bits - 2)
            turn = jnp.where(even, 2 * first + second, 2 * second + first)
            for i in range(2, bits):
                turn += ((row >> (bits - 1 - i)) & 1) << i
            at = pl.ds(pl.multiple_of(slot_low[leaf ^ turn] * sr, sr), sr)
            out[row * sr : (row + 1) * sr, :] = loads[at, :].astype(out.dtype)


def proj_kernel(mt, weighted, proj):
    proj[...] = jnp.dot(mt[...], weighted[...], preferred_element_type=F32).astype(BF16)


def proj_call(mt, weighted):
    (modes, rows), m = mt.shape, weighted.shape[1]
    return pl.pallas_call(
        proj_kernel,
        in_specs=[VMEM] * 2,
        out_specs=VMEM,
        out_shape=jax.ShapeDtypeStruct((modes, m), BF16),
        compiler_params=params(4),
        cost_estimate=cost(FILL, 2 * rows * m),
    )(mt, weighted)


def low_call(anc_low, ct, weighted, sr, leaves):
    rows, m = weighted.shape
    kept = leaves // 2 * sr
    low_rows = anc_low.shape[1] * sr
    return pl.pallas_call(
        functools.partial(low_kernel, leaves),
        in_specs=[SMEM, VMEM, VMEM],
        out_specs=[VMEM] * 2,
        out_shape=[jax.ShapeDtypeStruct((kept, m), F32), jax.ShapeDtypeStruct((kept, m), BF16)],
        scratch_shapes=[pltpu.SMEM((leaves,), jnp.int32), pltpu.VMEM((low_rows + sr, m), F32)],
        compiler_params=params(12),
        cost_estimate=cost(2 * m * rows * low_rows, 2 * rows * (low_rows + m)),
    )(anc_low, ct, weighted)


def part_kernel(n_got, keep, *refs):
    got, outs = refs[:n_got], refs[n_got:]
    height, width = outs[0].shape
    n = 0
    for r in range(keep.shape[0] // height):
        for c in range(keep.shape[1] // width):
            at = (slice(r * height, (r + 1) * height), slice(c * width, (c + 1) * width))
            total = keep[at]
            for g in got:
                total += g[at].astype(F32)
            outs[n][...] = total.astype(outs[n].dtype)
            n += 1


def part_call(keep, got, high, wide):
    piece = (keep.shape[0] // high, keep.shape[1] // wide)
    return pl.pallas_call(
        functools.partial(part_kernel, len(got)),
        in_specs=[VMEM] * (1 + len(got)),
        out_specs=[VMEM] * (high * wide),
        out_shape=[jax.ShapeDtypeStruct(piece, F32)] + [jax.ShapeDtypeStruct(piece, BF16)] * (high * wide - 1),
        compiler_params=params(4),
        cost_estimate=cost(keep.size, 8 * keep.size),
    )(keep, *got)


def quarter_kernel(keep, got, own, near, other, across):
    even = (lax.axis_index("group") & 1) == 0
    n = own.shape[0]
    for out, at in (
        (own, 0),
        (near, jnp.where(even, 2 * n, n)),
        (other, jnp.where(even, n, 2 * n)),
        (across, 3 * n),
    ):
        at = pl.ds(pl.multiple_of(at, n), n)
        out[...] = (keep[at, :] + got[at, :].astype(F32)).astype(out.dtype)


def quarter_call(keep, got):
    piece = (keep.shape[0] // 4, keep.shape[1])
    return pl.pallas_call(
        quarter_kernel,
        in_specs=[VMEM] * 2,
        out_specs=[VMEM] * 4,
        out_shape=[jax.ShapeDtypeStruct(piece, F32)] + [jax.ShapeDtypeStruct(piece, BF16)] * 3,
        compiler_params=params(4),
        cost_estimate=cost(keep.size, 8 * keep.size),
    )(keep, got)


def sum_kernel(keep, *refs):
    total = keep[...].astype(F32)
    for got in refs[:-1]:
        total += got[...].astype(F32)
    refs[-1][...] = total.astype(BF16)


def sum_call(keep, got):
    return pl.pallas_call(
        sum_kernel,
        in_specs=[VMEM] * (1 + len(got)),
        out_specs=VMEM,
        out_shape=jax.ShapeDtypeStruct(keep.shape, BF16),
        compiler_params=params(4),
        cost_estimate=cost(keep.size, 8 * keep.size),
    )(keep, *got)


def solve(kinv, loads):
    def parts(x):
        coarse = x.astype(BF16)
        fine = (x - coarse.astype(F32)).astype(BF16)
        return coarse, fine, (x - coarse.astype(F32) - fine.astype(F32)).astype(BF16)

    n = kinv.shape[0]
    total = None
    for i, part in enumerate(parts(loads) if loads.dtype == F32 else (loads,)):
        left = jnp.concatenate(parts(kinv)[: 3 - i], axis=0)
        product = jnp.dot(left, part, preferred_element_type=F32)
        for k in range(3 - i):
            term = product[k * n : (k + 1) * n]
            total = term if total is None else total + term
    return total


def low_end_kernel(kinv, keep, got, out):
    out[...] = solve(kinv[...], keep[...] + got[...].astype(F32))


def low_end_call(kinv, keep, got):
    return pl.pallas_call(
        low_end_kernel,
        in_specs=[VMEM] * 3,
        out_specs=VMEM,
        out_shape=jax.ShapeDtypeStruct(keep.shape, F32),
        compiler_params=params(4),
        cost_estimate=cost(12 * keep.size * 64, 8 * keep.size),
    )(kinv, keep, got)


def top_end_kernel(rels, kinv, *refs):
    parts, out, loads = refs[:-2], refs[-2], refs[-1]
    leaf = lax.axis_index("leaf")
    even = (lax.axis_index("group") & 1) == 0
    sr = kinv.shape[1]
    for part, (r_even, r_odd) in zip(parts, rels):
        height, width = part.shape
        there = leaf ^ jnp.where(even, r_even, r_odd)
        row = pl.multiple_of(((there >> 1) & 1) * height, height)
        col = pl.multiple_of((there & 1) * width, 128)
        loads[pl.ds(row, height), pl.ds(col, width)] = part[...]
    for b in range(out.shape[0] // sr):
        at = slice(b * sr, (b + 1) * sr)
        out[at, :] = solve(kinv[at, :], loads[at, :])


def top_end_call(parts, rels, kinv, m):
    rows = kinv.shape[0]
    return pl.pallas_call(
        functools.partial(top_end_kernel, rels),
        in_specs=[VMEM] * (1 + len(parts)),
        out_specs=VMEM,
        out_shape=jax.ShapeDtypeStruct((rows, m), F32),
        scratch_shapes=[pltpu.VMEM((rows, m), BF16)],
        compiler_params=params(8),
        cost_estimate=cost(12 * rows * m * 64, 8 * rows * m),
    )(kinv, *parts)


def per_device(
    top_modes, low_modes, anc_top, anc_low, coupling, leaf_mass, leaf_modes, leaf_coef, kinv_top, kinv_low
):
    sr = kinv_low.shape[1]
    m = low_modes.shape[1]
    leaves = lax.axis_size("leaf")
    near_top = send_group(top_modes, 1)
    far_low = send_leaf(low_modes, leaves // 2)
    near_top, to_send = lax.optimization_barrier((near_top, top_modes))
    far_top = send_group(to_send, 2)
    leaf_modes, mt = load_call((leaf_modes,), (True,))
    far_low, mt = lax.optimization_barrier((far_low, mt))
    held = gather_leaf(low_modes, far_low)
    coupling, ct = load_call((coupling,), (True,))
    tops = [top_modes, near_top, far_top, send_group(far_top, 1)]
    part = first_call(anc_top, tops, coupling, leaf_modes, leaf_coef, sr)
    send, keep, weighted = main_call(
        anc_top,
        anc_low,
        part,
        [h[0] for h in held],
        [h[1:] for h in held],
        coupling,
        leaf_mass,
        ct,
        sr,
        leaves,
        len(tops),
        top_modes.shape[0] // sr,
    )
    got = send_group(send, 1)
    low_keep, low_send = low_call(anc_low, ct, weighted, sr, leaves)
    low_keep, low_send, got = lax.optimization_barrier((low_keep, low_send, got))
    low_got = send_by_core(low_send, (0, 2), (0, 1))
    keep, send = part_call(keep, [got], 2, 1)
    send, weighted = lax.optimization_barrier((send, weighted))
    got = send_by_core(send, (2, 0), (0, 1))
    leaf_proj = proj_call(mt, weighted)
    got, leaf_proj = lax.optimization_barrier((got, leaf_proj))
    keep, near, other, across = quarter_call(keep, got)
    got = [send_by_core(x, *there) for x, *there in ((other, (0, 2), (2, 0)), (across, (0, 3), (2, 2)), (near, (0, 1), (0, 2)))]
    low_keep, got[0] = lax.optimization_barrier((low_keep, got[0]))
    low_keep, low_send = part_call(low_keep, [low_got], 2, 1)
    low_got = send_by_core(low_send, (0, 1), (0, 2))
    total = sum_call(keep, got)
    low_keep, total = lax.optimization_barrier((low_keep, total))
    for bit in range(2, leaves.bit_length() - 1):
        low_keep, low_send = part_call(low_keep, [low_got], 2, 1)
        low_got = send_leaf(low_send, 1 << bit)
        total = sum_call(total, [send_leaf(total, 1 << bit)])
    rels = ((0, 0), (3, 3), (2, 1), (1, 2))
    parts = [total] + [send_by_core(total, (0, even), (0, odd)) for even, odd in rels[1:]]
    new_low = low_end_call(kinv_low, low_keep, low_got)
    new_top = top_end_call(parts, rels, kinv_top, m)
    return (new_top, new_low, leaf_proj)


def solution(mesh):
    both = P(("group", "leaf"), None)
    return jax.shard_map(
        per_device,
        mesh=mesh,
        in_specs=(P("group", None), both, both, both, both, both, both, both, P("group", None), both),
        out_specs=(P("group", None), both, both),
        check_vma=False,
    )
```
